256 devices in a mesh: idx: 64 (over z, y, core), con: 4 (over x).
Axes of the slice: x: 4, y: 4, z: 8, core: 2. Of those that a mesh axis runs over, the one named last changes fastest.
Arguments:
- amplitude: bfloat16 [512, 8, 800], P('idx'), may hold values from -6 to 6
- pair_irrep: int32 [512], replicated, may hold values from 0 to 7
- fit_ac: bfloat16 [1024, 64, 8], P('con'), may hold values from -6 to 6
- fitting_tensor_bd: bfloat16 [1024, 1024, 800], P('con', 'idx'), may hold values from -0.0068359375 to 0.0068359375
- a_irrep: int32 [64], replicated, may hold values from 0 to 7
- c_irrep: int32 [8], replicated, may hold values from 0 to 7
- irrep_start: int32 [8], replicated, may hold values from 0 to 640, as said below
- product: int32 [8, 8], replicated, may hold values from 0 to 7, as said below
- tile_len: int32 [64], replicated, may hold values from 1 to 16, 800 in all
- tile_irrep: int32 [64], replicated, may hold values from 0 to 7
Outputs:
- residual: float32 [512, 64, 1024], P(('idx', 'con'))
The draws below stay inside these ranges and needn't reach their ends.
Inputs may be any that keep to these rules, and one draw needn't show every extreme that they name: Irrep blocks are contiguous in d, in order of g; each holds at least one orbital and at most 160; the last block holds exactly 160; irrep_start[0] is 0. product is the table of a commutative group in which every element is its own inverse. `tile_len`: the tile lengths sum to 800; some tile is full.
All inputs are finite; a program needn't handle non-finite values.
Results may differ from the reference program's by a relative error of at most 0.0029.
Values may be sent and summed in bfloat16 or wider, within the bound.
A program may use at most 192 MiB of HBM per device.

```python
import math
import jax
import jax.numpy as jnp
import numpy as np
from jax import lax

VIRTUAL_COUNT = 800
FITTING_COUNT = 1024
NIRR = 8
BW = 16
NTILE = 64
VA = 64
VC = 8
P_SIZE = 512
TILE_SLOT_COUNT = 1024
N_CON = 4


def draw_irrep_start(key, part):
    key = jax.random.fold_in(key, 11)
    widest = VIRTUAL_COUNT // 5
    others_total = VIRTUAL_COUNT - widest
    base = others_total // (NIRR - 1)
    extra = others_total - base * (NIRR - 1)
    others = jnp.full((NIRR - 1,), base, jnp.int32) + (jnp.arange(NIRR - 1) < extra).astype(jnp.int32)
    moves = jax.random.randint(key, (NIRR - 1,), 0, base // 3 + 1).astype(jnp.int32)
    others = others + moves - jnp.roll(moves, 1)
    sizes = jnp.concatenate([others, jnp.array([widest], jnp.int32)])
    return (jnp.cumsum(sizes) - sizes).astype(jnp.int32)


def draw_product(key, part):
    key = jax.random.fold_in(key, 23)
    order = jax.random.permutation(key, NIRR).astype(jnp.int32)
    inverse = jnp.argsort(order).astype(jnp.int32)
    mixed = jnp.bitwise_xor(inverse[:, None], inverse[None, :])
    return order[mixed].astype(jnp.int32)


def place_ends(drawn, own_key, low, top_value):
    index_at = [jax.random.randint(jax.random.fold_in(own_key, axis), (), 0, length) for axis, length in enumerate(drawn.shape)]
    widest = drawn.shape.index(max(drawn.shape))
    next_to = index_at[:widest] + [(index_at[widest] + 1) % drawn.shape[widest]] + index_at[widest + 1:]
    return drawn.at[tuple(index_at)].set(low).at[tuple(next_to)].set(top_value)


def shard_levels(rng, dims, shards, low, largest):
    gain = 1.0
    for dim, blocks in shards:
        heights = jax.random.uniform(jax.random.fold_in(jax.random.fold_in(rng, 6), dim), (blocks,), jnp.float32, low / len(shards), largest / len(shards))
        gain = gain * jnp.repeat(jnp.exp(heights), dims[dim] // blocks).reshape((-1,) + (1,) * (len(dims) - 1 - dim))
    return gain


def split_up(amount, total, most, skew):
    weights = [(1 << 20) // math.isqrt(grade ** skew) + 1 for grade in range(2, amount + 1)]
    spare, given = total - most - (amount - 1), [1] * (amount - 1)
    while spare > 0:
        free = [i for i in range(amount - 1) if given[i] < most]
        mass, remaining = sum([weights[i] for i in free]), spare
        for i in free:
            addition = min(most - given[i], max(1, remaining * weights[i] // mass), spare)
            given[i] = given[i] + addition
            spare = spare - addition
    return np.array([most] + given)


def uneven(own_key, number_of, total, reach, lean):
    if number_of == 2:
        one = jax.random.randint(own_key, (), max(1, total - reach), min(reach, total - 1) + 1)
        return jnp.stack([one, total - one])
    lengths = jnp.asarray(split_up(number_of, total, reach, lean), jnp.int32)
    pairs = (number_of - 1) // 2
    source_of, taker = lengths[1:1 + 2 * pairs:2], lengths[2:2 + 2 * pairs:2]
    margin = jnp.minimum(source_of - 1, reach - taker)
    shifted = jax.random.randint(jax.random.fold_in(own_key, 1), (pairs,), 0, 1 << 20) % (margin + 1)
    lengths = lengths.at[1:1 + 2 * pairs:2].set(source_of - shifted).at[2:2 + 2 * pairs:2].set(taker + shifted)
    return lengths[jax.random.permutation(jax.random.fold_in(own_key, 2), number_of)]


def noise(key, shape, scale, most, split=(), held_as=jnp.bfloat16):
    gain = shard_levels(key, shape, split, -0.22, 0.18) if split else 1.0
    drawn = jax.random.normal(key, shape, jnp.float32) * scale * gain
    return jnp.minimum(jnp.maximum(drawn, -most), most).astype(held_as)


def setup_inputs(seed: int = 0) -> dict:
    splits = jax.random.split(jax.random.key(seed), 11)
    return {
        "amplitude": noise(splits[0], (P_SIZE, VC, VIRTUAL_COUNT), 1.0, 6.0, ((0, 64),)),
        "pair_irrep": place_ends(jax.random.randint(splits[1], (P_SIZE,), 0, NIRR), jax.random.fold_in(splits[1], 1), 0, NIRR - 1).astype(jnp.int32),
        "fit_ac": noise(splits[2], (FITTING_COUNT, VA, VC), 1.0, 6.0, ((0, 4),)),
        "fitting_tensor_bd": noise(splits[3], (FITTING_COUNT, TILE_SLOT_COUNT, VIRTUAL_COUNT), (FITTING_COUNT * VIRTUAL_COUNT) ** -0.5, 0.0068359375, ((0, 4), (1, 64))),
        "a_irrep": place_ends(jax.random.randint(splits[4], (VA,), 0, NIRR), jax.random.fold_in(splits[4], 1), 0, NIRR - 1).astype(jnp.int32),
        "c_irrep": place_ends(jax.random.randint(splits[5], (VC,), 0, NIRR), jax.random.fold_in(splits[5], 1), 0, NIRR - 1).astype(jnp.int32),
        "irrep_start": draw_irrep_start(jax.random.fold_in(splits[10], 71), 0),
        "product": draw_product(jax.random.fold_in(splits[10], 71), 0),
        "tile_len": uneven(splits[8], NTILE, VIRTUAL_COUNT, BW, 1).astype(jnp.int32),
        "tile_irrep": place_ends(jax.random.randint(splits[9], (NTILE,), 0, NIRR), jax.random.fold_in(splits[9], 1), 0, NIRR - 1).astype(jnp.int32),
    }


def orbital_irreps(irrep_start, width):
    spots = jnp.arange(width, dtype=jnp.int32)
    return jnp.sum((spots[:, None] >= irrep_start[None, :]).astype(jnp.int32), axis=1) - 1


def reference(amplitude, pair_irrep, fit_ac, fitting_tensor_bd, a_irrep, c_irrep, irrep_start, product, tile_len, tile_irrep):
    d_irrep = orbital_irreps(irrep_start, VIRTUAL_COUNT)
    target = product[pair_irrep[:, None], c_irrep[None, :]]
    masked = jnp.where(d_irrep[None, None, :] == target[:, :, None], amplitude, jnp.zeros_like(amplitude))
    dense = masked.astype(jnp.float32)
    share = FITTING_COUNT // N_CON

    def one_tile(tile):
        rows = lax.dynamic_slice_in_dim(fitting_tensor_bd, tile * BW, BW, 1)
        total = jnp.zeros((P_SIZE, VA, BW), jnp.float32)
        for slice_no in range(N_CON):
            left = fit_ac[slice_no * share:(slice_no + 1) * share].astype(jnp.float32)
            right = rows[slice_no * share:(slice_no + 1) * share].astype(jnp.float32)
            fitted_result = jnp.einsum("qac,qbd->acbd", left, right, precision=lax.Precision.HIGHEST).astype(jnp.bfloat16)
            fitted_result = lax.optimization_barrier(fitted_result).astype(jnp.float32)
            total = total + jnp.einsum("pcd,acbd->pab", dense, fitted_result, precision=lax.Precision.HIGHEST)
        return total

    blocks = lax.map(one_tile, jnp.arange(NTILE, dtype=jnp.int32))
    ladder = jnp.transpose(blocks, (1, 2, 0, 3)).reshape(P_SIZE, VA, NTILE * BW)
    slots = jnp.arange(NTILE * BW, dtype=jnp.int32)
    live = (slots % BW) < jnp.repeat(tile_len, BW)
    b_irrep = jnp.repeat(tile_irrep, BW)
    pair_ab = product[a_irrep[:, None], b_irrep[None, :]]
    keep = (pair_ab[None, :, :] == pair_irrep[:, None, None]) & live[None, None, :]
    return jnp.where(keep, ladder, jnp.zeros_like(ladder))
```

```python
import functools

import jax
import jax.numpy as jnp
from jax import lax
from jax.experimental import pallas as pl
from jax.experimental.pallas import tpu as pltpu
from jax.sharding import PartitionSpec as P

MESH = pl.DeviceIdType.MESH
BW = 16
NIRR = 8
WIN = 192
SLOTS = 16
NV = 800
KDIM = 8 * WIN
F32 = jnp.float32
BF16 = jnp.bfloat16


def nt_dot(left, right):
    return lax.dot_general(left, right, (((1,), (1,)), ((), ())), preferred_element_type=F32)


def lookup(index, entries):
    out = jnp.zeros_like(index)
    for spot, entry in enumerate(entries):
        out = jnp.where(index == spot, entry, out)
    return out


def ladder_kernel(
    pair_s, airr_s, cirr_s, start_s, prod_s, tirr_s, round_s,
    amp_ref, a_ref, pairs_ref, f_hbm,
    out_ref,
    fv, x32, tc, tsend, trecv, g_ref, asel, d_ref, rhs, rneed, acc, xf, xb, xr, m_ref, v0, v1,
    fsem, tsib_s, tsib_r, y_s, y_r, rr_s, rr_r, rl_s, rl_r, sib_s, sib_r, x_s, x_r, a_s, a_r, v_s, v_r,
):
    idx = lax.axis_index("idx")
    con = lax.axis_index("con")
    core = lax.rem(idx, 2)
    chip = idx // 2
    y = lax.rem(chip, 4)
    z = chip // 4
    sibling = (chip * 2 + 1 - core, con)

    def chip_at(zz, yy):
        return ((zz * 4 + yy) * 2 + core, con)

    for b in range(16):
        pltpu.make_async_copy(f_hbm.at[b], fv.at[b], fsem.at[b]).start()

    barrier = pltpu.get_barrier_semaphore()
    pl.semaphore_signal(barrier, inc=1, device_id=sibling, device_id_type=MESH)

    def greet(j, carry):
        other = lax.rem(chip + j, 32)
        pl.semaphore_signal(barrier, inc=1, device_id=(other * 2 + core, con), device_id_type=MESH)
        return carry

    lax.fori_loop(1, 32, greet, 0)
    for s in range(1, 4):
        pl.semaphore_signal(barrier, inc=1, device_id=(idx, lax.rem(con + s, 4)), device_id_type=MESH)

    first = [jnp.minimum(start_s[g] // 32, (NV - WIN) // 32) for g in range(NIRR)]
    base = [first[g] * 32 for g in range(NIRR)]
    low = [start_s[g] - base[g] for g in range(NIRR)]
    high = [(start_s[g + 1] if g < 7 else NV) - base[g] for g in range(NIRR)]
    x32[:, 768:896] = jnp.zeros((64, 128), F32)
    x32[:, 0:NV] = amp_ref[...].astype(F32).reshape(64, NV)
    rows8 = lax.broadcasted_iota(jnp.int32, (8, 128), 0)
    target = []
    for p in range(8):
        irr = pair_s[idx * 8 + p]
        part = jnp.zeros((8, 128), jnp.int32)
        for c in range(8):
            part = jnp.where(rows8 == c, prod_s[irr, cirr_s[c]], part)
        target.append(part)
    target = jnp.concatenate(target, axis=0)
    target = jnp.concatenate([target, target], axis=1)
    lanes = lax.broadcasted_iota(jnp.int32, (64, 256), 1)
    window = jnp.zeros((64, 256), F32)
    whole = x32[...]
    for g in range(NIRR):
        moved = pltpu.roll(whole, 896 - base[g], 1)[:, 0:256]
        window = jnp.where((target == g) & (lanes >= low[g]) & (lanes < high[g]), moved, window)
    tc[0, :, :] = window[:, 0:128]
    tc[1, :, :] = window[:, 128:256]
    lane8 = lax.broadcasted_iota(jnp.int32, (8, 128), 1)
    for c in range(8):
        tsend[:, c * 128:(c + 1) * 128] = tc[0, pl.ds(c, 8, stride=8), :]
    for m in range(4):
        even = tc[1, pl.ds(2 * m, 8, stride=8), :]
        odd = pltpu.roll(tc[1, pl.ds(2 * m + 1, 8, stride=8), :], 64, 1)
        tsend[:, 1024 + m * 128:1024 + (m + 1) * 128] = jnp.where(lane8 < 64, even, odd)

    pl.semaphore_wait(barrier, 35)
    tcopy = pltpu.make_async_remote_copy(
        src_ref=tsend, dst_ref=trecv, send_sem=tsib_s, recv_sem=tsib_r, device_id=sibling, device_id_type=MESH)
    tcopy.start()

    tile = tirr_s[idx]
    prow = [[prod_s[i, j] for j in range(8)] for i in range(8)]
    ptile = [prod_s[i, tile] for i in range(8)]
    n = lax.broadcasted_iota(jnp.int32, (8, 512), 1)
    a_of, c_of = n // 8, lax.rem(n, 8)
    a_lane = lookup(a_of, [airr_s[a] for a in range(64)])
    c_lane = lookup(c_of, [cirr_s[c] for c in range(8)])
    a_rows = []
    for k in range(8):
        part = jnp.zeros((8, 128), jnp.int32)
        for i in range(8):
            part = jnp.where(rows8 == i, airr_s[k * 8 + i], part)
        a_rows.append(part)
    rank = jnp.zeros((8, 512), jnp.int32)
    for k in range(8):
        other = jnp.concatenate([a_rows[k]] * 4, axis=1)
        rank = rank + jnp.where((other == a_lane) & (lax.broadcasted_iota(jnp.int32, (8, 512), 0) + k * 8 < a_of), 1, 0)
    rank = jnp.sum(rank, axis=0, keepdims=True) - round_s[0] * SLOTS
    block = lookup(lookup(a_lane, ptile) * 8 + c_lane, [e for row in prow for e in row])[0:1]
    code = jnp.where((rank >= 0) & (rank < SLOTS), block * 128 + c_of[0:1] * SLOTS + rank, -1)
    spot = lax.broadcasted_iota(jnp.int32, (128, 512), 0)
    for g in range(NIRR):
        pick = jnp.where(spot + g * 128 == code, 1.0, 0.0).astype(BF16)
        asel[g, :, :] = jnp.dot(pick, a_ref[...], preferred_element_type=F32).astype(BF16)

    need = lookup(lookup(pairs_ref[...], ptile), list(range(8))).astype(F32)
    eye = lax.broadcasted_iota(jnp.int32, (128, 128), 0) == lax.broadcasted_iota(jnp.int32, (128, 128), 1)
    for k in range(4):
        column = jnp.sum(jnp.where(eye, need[k:k + 1, :], 0.0), axis=1, keepdims=True)
        rneed[pl.ds(k * 128, 128), :] = jnp.broadcast_to(column, (128, 128))

    def integrals(begin, end):
        def one(b, carry):
            for g in range(NIRR):
                main = fv[b, pl.ds(first[g], 6), :, :].reshape(WIN, 256)
                tail = fv[b, pl.ds(first[g] + 4, 2), :, :].reshape(64, 256)
                got = nt_dot(asel[g], jnp.concatenate([main, tail], axis=0))
                d_ref[g, :, pl.ds(pl.multiple_of(b * 16, 16), 16), :] = got.astype(BF16).reshape(8, 16, 256)
            return carry

        lax.fori_loop(begin, end, one, 0)

    half = pl.ds(pl.multiple_of(core * 768, 128), 768)

    def group(zz):
        return g_ref.at[pl.ds(pl.multiple_of(lax.rem(zz + 8, 8) * 64, 64), 64), half]

    def to_sibling(slot, zz):
        part = group(zz)
        return pltpu.make_async_remote_copy(
            src_ref=part, dst_ref=part, send_sem=sib_s.at[slot], recv_sem=sib_r.at[slot], device_id=sibling, device_id_type=MESH)

    def ring(zz, to, send, recv):
        part = group(zz)
        return pltpu.make_async_remote_copy(
            src_ref=part, dst_ref=part, send_sem=send, recv_sem=recv, device_id=chip_at(lax.rem(to + 8, 8), y), device_id_type=MESH)

    def right(s):
        return ring(z - s, z + 1, rr_s.at[s], rr_r.at[s])

    def right_in(s):
        return ring(z - 1 - s, z + 1, rr_s.at[s], rr_r.at[s])

    def left(s):
        return ring(z + s, z - 1, rl_s.at[s], rl_r.at[s])

    def left_in(s):
        return ring(z + 1 + s, z - 1, rl_s.at[s], rl_r.at[s])

    for b in range(16):
        pltpu.make_async_copy(f_hbm.at[b], fv.at[b], fsem.at[b]).wait()
    integrals(0, 1)
    tcopy.wait()
    own, other = tsend[...], trecv[...]
    top = jnp.where(core == 0, own[:, 0:768], other[:, 768:KDIM])
    bottom = jnp.where(core == 0, other[:, 0:768], own[:, 768:KDIM])
    mine = pl.ds(pl.multiple_of(chip * 16, 16), 16)
    g_ref[mine, half] = jnp.concatenate([top, bottom], axis=0).astype(BF16)

    def along_y(s):
        part = g_ref.at[mine, half]
        return pltpu.make_async_remote_copy(
            src_ref=part, dst_ref=part, send_sem=y_s.at[s - 1], recv_sem=y_r.at[s - 1],
            device_id=chip_at(z, lax.rem(y + s, 4)), device_id_type=MESH)

    def along_y_in(s):
        part = g_ref.at[pl.ds(pl.multiple_of((z * 4 + lax.rem(y + 4 - s, 4)) * 16, 16), 16), half]
        return pltpu.make_async_remote_copy(
            src_ref=part, dst_ref=part, send_sem=y_s.at[s - 1], recv_sem=y_r.at[s - 1],
            device_id=chip_at(z, lax.rem(y + s, 4)), device_id_type=MESH)

    for s in range(1, 4):
        along_y(s).start()
    integrals(1, 3)
    for s in range(1, 4):
        along_y_in(s).wait_recv()
    right(0).start()
    left(0).start()
    to_sibling(0, z).start()
    integrals(3, 6)
    right_in(0).wait_recv()
    right(1).start()
    left_in(0).wait_recv()
    left(1).start()
    to_sibling(1, z - 1).start()
    to_sibling(2, z + 1).start()
    integrals(6, 10)
    right_in(1).wait_recv()
    right(2).start()
    left_in(1).wait_recv()
    left(2).start()
    to_sibling(3, z - 2).start()
    to_sibling(4, z + 2).start()
    integrals(10, 14)
    right_in(2).wait_recv()
    right(3).start()
    left_in(2).wait_recv()
    to_sibling(5, z - 3).start()
    to_sibling(6, z + 3).start()
    integrals(14, 16)
    right_in(3).wait_recv()
    to_sibling(7, z - 4).start()

    other_half = pl.ds(pl.multiple_of((1 - core) * 768, 128), 768)
    for slot, away in enumerate((0, -1, 1, -2, 2, -3, 3, -4)):
        part = g_ref.at[pl.ds(pl.multiple_of(lax.rem(z + away + 8, 8) * 64, 64), 64), other_half]
        pltpu.make_async_remote_copy(
            src_ref=part, dst_ref=part, send_sem=sib_s.at[slot], recv_sem=sib_r.at[slot], device_id=sibling,
            device_id_type=MESH).wait_recv()

    acc[...] = jnp.zeros_like(acc)
    lane256 = lax.broadcasted_iota(jnp.int32, (256, 128), 1)

    def one_irrep(r, carry):
        pair_irr = prod_s[r, tile]
        blocks = [prod_s[pair_irr, cirr_s[c]] for c in range(8)]
        for c in range(8):
            rhs[:, c * 128:(c + 1) * 128] = d_ref[blocks[c], c, :, 0:128]
        for m in range(4):
            even = d_ref[blocks[2 * m], 2 * m, :, 128:256]
            odd = d_ref[blocks[2 * m + 1], 2 * m + 1, :, 128:256]
            rhs[:, 1024 + m * 128:1024 + (m + 1) * 128] = jnp.where(lane256 < 64, even, odd)
        for k in range(2):
            rows = pl.ds(k * 256, 256)
            got = nt_dot(g_ref[rows, :], rhs[...])
            hit = rneed[rows, :] == r.astype(F32)
            for h in range(2):
                acc[h, rows, :] = jnp.where(hit, got[:, h * 128:(h + 1) * 128], acc[h, rows, :])
        return carry

    lax.fori_loop(0, NIRR, one_irrep, 0)

    for r in range(4):
        for q in range(4):
            for h in range(2):
                for cg in range(4):
                    xf[r, pl.ds(cg * 64 + q * 2 + h, 8, stride=8), :] = acc[
                        h, pl.ds(cg * 128 + (q // 2) * 8 + r * 2 + q % 2, 8, stride=16), :]
        xb[r, :, :] = xf[r, :, :].astype(BF16)

    def along_x(s):
        to = lax.rem(con + s, 4)
        return pltpu.make_async_remote_copy(
            src_ref=xb.at[to], dst_ref=xr.at[s - 1], send_sem=x_s.at[s - 1], recv_sem=x_r.at[s - 1],
            device_id=(idx, to), device_id_type=MESH)

    for s in range(1, 4):
        along_x(s).start()
    for s in range(1, 4):
        along_x(s).wait_recv()
    m_ref[...] = xf[con, :, :] + (xr[0].astype(F32) + xr[1].astype(F32) + xr[2].astype(F32))

    here = pl.ds(pl.multiple_of(chip * 8, 8), 8)

    def give(j, carry):
        other_chip = lax.rem(chip + j, 32)
        pltpu.make_async_remote_copy(
            src_ref=m_ref.at[pl.ds(pl.multiple_of(other_chip * 8, 8), 8), :], dst_ref=v0.at[here, :], send_sem=a_s, recv_sem=a_r,
            device_id=(other_chip * 2 + core, con), device_id_type=MESH).start()
        return carry

    lax.fori_loop(1, 32, give, 0)
    v0[here, :] = m_ref[here, :]
    many = v0.at[0:248, :]
    pltpu.make_async_copy(many, many, a_r).wait()
    vcopy = pltpu.make_async_remote_copy(
        src_ref=v0, dst_ref=v1, send_sem=v_s, recv_sem=v_r, device_id=sibling, device_id_type=MESH)
    vcopy.start()
    out_ref[core, :, :] = v0[...]
    pltpu.make_async_copy(many, many, a_s).wait()
    for s in range(1, 4):
        along_y(s).wait_send()
        along_x(s).wait_send()
    for s in range(4):
        right(s).wait_send()
    for s in range(3):
        left(s).wait_send()
    for slot in range(8):
        to_sibling(slot, z).wait_send()
    vcopy.wait()
    out_ref[1 - core, :, :] = v1[...]


def place_kernel(
    pair_s, prod_s, round_s, airr_ref, tlen_ref, tirr_ref, v_ref, prev_ref, out_ref, left, expand, *, first_round
):
    idx = lax.axis_index("idx")
    con = lax.axis_index("con")
    core = lax.rem(idx, 2)
    lane16 = lax.broadcasted_iota(jnp.int32, (16, 128), 1)
    for h in range(2):
        parts = []
        for pp in range(2):
            for kappa in range(2):
                parts.append(v_ref[kappa, pl.ds(core * 4 + pp * 2 + h, 32, stride=8), :])
        turned = jnp.concatenate(parts, axis=0).T
        for bl in range(8):
            piece = turned[bl * 16:(bl + 1) * 16, :]
            for pp in range(2):
                kept = jnp.where((lane16 // 64) == pp, piece, 0.0)
                left[pl.ds(pp * 16, 16), (h * 8 + bl) * 128:(h * 8 + bl + 1) * 128] = kept
    source = lax.broadcasted_iota(jnp.int32, (128, 1024), 0)
    lane = lax.broadcasted_iota(jnp.int32, (128, 1024), 1)
    local = lax.rem(source, 64)
    tile_first = (lax.rem(local, 32) * 2 + local // 32) * 16
    for b in range(16):
        expand[b * 128:(b + 1) * 128, :] = jnp.where(tile_first + b == lane, 1.0, 0.0).astype(BF16)
    a_row = airr_ref[...]
    row = lax.broadcasted_iota(jnp.int32, (64, 64), 0)
    col = lax.broadcasted_iota(jnp.int32, (64, 64), 1)
    a_col = jnp.sum(jnp.where(row == col, a_row, 0), axis=1, keepdims=True)
    rank = jnp.sum(jnp.where((a_col == a_row) & (col < row), 1, 0), axis=1, keepdims=True) - round_s[0] * SLOTS
    slot = lax.broadcasted_iota(jnp.int32, (64, 32), 1)
    full = left[...]
    big = full.astype(BF16)
    small = (full - big.astype(F32)).astype(BF16)
    held = (rank >= 0) & (rank < SLOTS)
    pick = [jnp.where(held & (slot == rank + pp * 16), 1.0, 0.0) for pp in range(2)]
    pick = jnp.concatenate(pick, axis=0).astype(BF16)
    table = expand[...]

    def placed(part):
        chosen = jnp.dot(pick, part, preferred_element_type=F32).astype(BF16)
        return jnp.dot(chosen, table, preferred_element_type=F32)

    values = placed(big) + placed(small)
    spread = jnp.where(
        lax.broadcasted_iota(jnp.int32, (64, 1024), 0) == lax.broadcasted_iota(jnp.int32, (64, 1024), 1) // 16, 1.0, 0.0
    ).astype(BF16)

    def lanes_of(ref):
        wide = jnp.broadcast_to(ref[...], (8, 64)).astype(F32).astype(BF16)
        return jnp.dot(wide, spread, preferred_element_type=F32)[0:1]

    length, irrep = lanes_of(tlen_ref), lanes_of(tirr_ref).astype(jnp.int32)
    live = lax.rem(lax.broadcasted_iota(jnp.int32, (1, 1024), 1), 16).astype(F32) < length
    for pp in range(2):
        pair_irr = pair_s[idx * 8 + con * 2 + pp]
        need = lookup(irrep, [prod_s[pair_irr, i] for i in range(8)])
        need = jnp.where(live, need, -1)
        keep = a_col == need
        got = jnp.where(keep, values[pp * 64:(pp + 1) * 64, :], 0.0)
        if not first_round:
            got = got + prev_ref[pp, :, :]
        out_ref[pp, :, :] = got


def smem():
    return pl.BlockSpec(memory_space=pltpu.SMEM)


def vmem():
    return pl.BlockSpec(memory_space=pltpu.VMEM)


def ladder(pair_irrep, a_irrep, c_irrep, irrep_start, product, tile_irrep, number, amplitude, fit, pairs, fitting):
    dma = pltpu.SemaphoreType.DMA
    return pl.pallas_call(
        ladder_kernel,
        out_shape=jax.ShapeDtypeStruct((2, 256, 128), F32),
        in_specs=[smem()] * 7 + [vmem()] * 3 + [pl.BlockSpec(memory_space=pltpu.HBM)],
        out_specs=vmem(),
        scratch_shapes=[
            pltpu.VMEM((16, 25, 32, 256), BF16),
            pltpu.VMEM((64, 896), F32),
            pltpu.VMEM((2, 64, 128), F32),
            pltpu.VMEM((8, KDIM), F32),
            pltpu.VMEM((8, KDIM), F32),
            pltpu.VMEM((512, KDIM), BF16),
            pltpu.VMEM((NIRR, 128, 256), BF16),
            pltpu.VMEM((NIRR, 8, 256, 256), BF16),
            pltpu.VMEM((256, KDIM), BF16),
            pltpu.VMEM((512, 128), F32),
            pltpu.VMEM((2, 512, 128), F32),
            pltpu.VMEM((4, 256, 128), F32),
            pltpu.VMEM((4, 256, 128), BF16),
            pltpu.VMEM((3, 256, 128), BF16),
            pltpu.VMEM((256, 128), F32),
            pltpu.VMEM((256, 128), F32),
            pltpu.VMEM((256, 128), F32),
            dma((16,)), dma, dma, dma((3,)), dma((3,)), dma((4,)), dma((4,)), dma((3,)), dma((3,)),
            dma((8,)), dma((8,)), dma((3,)), dma((3,)), dma, dma, dma, dma,
        ],
        compiler_params=pltpu.CompilerParams(
            collective_id=0, has_side_effects=True, vmem_limit_bytes=48 * 1024 * 1024),
        name="ladder",
    )(pair_irrep, a_irrep, c_irrep, irrep_start, product, tile_irrep, number, amplitude, fit, pairs, fitting)


def place(pair_irrep, product, number, a_irrep, tile_len, tile_irrep, gathered, previous, first_round):
    return pl.pallas_call(
        functools.partial(place_kernel, first_round=first_round),
        out_shape=jax.ShapeDtypeStruct((2, 64, 1024), F32),
        in_specs=[smem()] * 3 + [vmem()] * 5,
        out_specs=vmem(),
        scratch_shapes=[pltpu.VMEM((32, 2048), F32), pltpu.VMEM((2048, 1024), BF16)],
        compiler_params=pltpu.CompilerParams(vmem_limit_bytes=48 * 1024 * 1024),
        name="place" if first_round else "place_more",
    )(pair_irrep, product, number, a_irrep, tile_len, tile_irrep, gathered, previous)


def body(
    amplitude, pair_irrep, fit_ac, fitting_tensor_bd, a_irrep, c_irrep, irrep_start, product, tile_len, tile_irrep
):
    fitting = jnp.transpose(fitting_tensor_bd, (1, 2, 0)).reshape(16, 25, 32, 256)
    fit = jnp.transpose(fit_ac, (1, 2, 0)).reshape(512, 256)
    pairs = pair_irrep.reshape(4, 128)
    a_row, len_row, irr_row = a_irrep.reshape(1, 64), tile_len.reshape(1, 64), tile_irrep.reshape(1, 64)
    counts = jnp.sum((a_irrep[:, None] == jnp.arange(NIRR, dtype=jnp.int32)[None, :]).astype(jnp.int32), axis=0)
    rounds = (jnp.max(counts) + SLOTS - 1) // SLOTS

    def one_round(number, previous, first_round):
        number = jnp.asarray(number, jnp.int32).reshape(1)
        gathered = ladder(
            pair_irrep, a_irrep, c_irrep, irrep_start, product, tile_irrep, number, amplitude, fit, pairs, fitting)
        return place(pair_irrep, product, number, a_row, len_row, irr_row, gathered, previous, first_round)

    out = one_round(0, jnp.zeros((2, 64, 1024), F32), False)

    def more(carry):
        return carry[0] < rounds

    def step(carry):
        number, out = carry
        return number + 1, one_round(number, out, False)

    return lax.while_loop(more, step, (jnp.int32(1), out))[1]


def solution(mesh):
    placed = (
        P("idx", None, None),
        P(),
        P("con", None, None),
        P("con", "idx", None),
        P(),
        P(),
        P(),
        P(),
        P(),
        P(),
    )
    return jax.shard_map(
        body, mesh=mesh, in_specs=placed, out_specs=P(("idx", "con"), None, None), check_vma=False
    )
```

```python
import functools

import jax
import jax.numpy as jnp
from jax import lax
from jax.experimental import pallas as pl
from jax.experimental.pallas import tpu as pltpu
from jax.sharding import PartitionSpec as P

MESH = pl.DeviceIdType.MESH
BW = 16
NIRR = 8
WIN = 192
SLOTS = 16
NV = 800
KDIM = 8 * WIN
CUT = 384
F32 = jnp.float32
BF16 = jnp.bfloat16


def nt_dot(left, right):
    return lax.dot_general(left, right, (((1,), (1,)), ((), ())), preferred_element_type=F32)


def lookup(index, entries):
    out = jnp.zeros_like(index)
    for spot, entry in enumerate(entries):
        out = jnp.where(index == spot, entry, out)
    return out


def ladder_kernel(
    pair_s, airr_s, cirr_s, start_s, prod_s, tirr_s, round_s,
    amp_ref, a_ref, pairs_ref, f_hbm,
    out_ref,
    fv, x32, tc, tsend, trecv, g_ref, asel, d_ref, rhs, rneed, acc, xf, xb, xr, zf, zb, vb,
    fsem, tsib_s, tsib_r, y_s, y_r, rr_s, rr_r, rl_s, rl_r, sib_s, sib_r, zg_s, zg_r, side_s, side_r, on_s, on_r,
    x_s, x_r, ze_s, ze_r,
):
    idx = lax.axis_index("idx")
    con = lax.axis_index("con")
    core = lax.rem(idx, 2)
    chip = idx // 2
    y = lax.rem(chip, 4)
    z = chip // 4
    sibling = (chip * 2 + 1 - core, con)

    def at_y(dy):
        return ((z * 4 + lax.rem(y + dy + 4, 4)) * 2 + core, con)

    def at_z(dz):
        return ((lax.rem(z + dz + 8, 8) * 4 + y) * 2 + core, con)

    def at_x(dx):
        return (idx, lax.rem(con + dx, 4))

    def remote(src, dst, send, recv, to):
        return pltpu.make_async_remote_copy(
            src_ref=src, dst_ref=dst, send_sem=send, recv_sem=recv, device_id=to, device_id_type=MESH)

    for b in range(16):
        pltpu.make_async_copy(f_hbm.at[b], fv.at[b], fsem.at[b]).start()

    barrier = pltpu.get_barrier_semaphore()
    peers = [sibling]
    for s in range(1, 8):
        there = lax.rem(z + s, 8) * 4 + y
        peers += [(there * 2 + core, con), (there * 2 + 1 - core, con)]
    for s in range(4):
        for dx in range(4):
            if s or dx:
                peers.append(((z * 4 + lax.rem(y + s, 4)) * 2 + core, lax.rem(con + dx, 4)))
    for peer in peers:
        pl.semaphore_signal(barrier, inc=1, device_id=peer, device_id_type=MESH)

    first = [jnp.minimum(start_s[g] // 32, (NV - WIN) // 32) for g in range(NIRR)]
    base = [first[g] * 32 for g in range(NIRR)]
    low = [start_s[g] - base[g] for g in range(NIRR)]
    high = [(start_s[g + 1] if g < 7 else NV) - base[g] for g in range(NIRR)]
    x32[:, 768:896] = jnp.zeros((64, 128), F32)
    x32[:, 0:NV] = amp_ref[...].astype(F32).reshape(64, NV)
    rows8 = lax.broadcasted_iota(jnp.int32, (8, 128), 0)
    target = []
    for p in range(8):
        irr = pair_s[idx * 8 + p]
        part = jnp.zeros((8, 128), jnp.int32)
        for c in range(8):
            part = jnp.where(rows8 == c, prod_s[irr, cirr_s[c]], part)
        target.append(part)
    target = jnp.concatenate(target, axis=0)
    target = jnp.concatenate([target, target], axis=1)
    lanes = lax.broadcasted_iota(jnp.int32, (64, 256), 1)
    window = jnp.zeros((64, 256), F32)
    whole = x32[...]
    for g in range(NIRR):
        moved = pltpu.roll(whole, 896 - base[g], 1)[:, 0:256]
        window = jnp.where((target == g) & (lanes >= low[g]) & (lanes < high[g]), moved, window)
    tc[0, :, :] = window[:, 0:128]
    tc[1, :, :] = window[:, 128:256]
    lane8 = lax.broadcasted_iota(jnp.int32, (8, 128), 1)
    for c in range(8):
        tsend[:, c * 128:(c + 1) * 128] = tc[0, pl.ds(c, 8, stride=8), :]
    for m in range(4):
        even = tc[1, pl.ds(2 * m, 8, stride=8), :]
        odd = pltpu.roll(tc[1, pl.ds(2 * m + 1, 8, stride=8), :], 64, 1)
        tsend[:, 1024 + m * 128:1024 + (m + 1) * 128] = jnp.where(lane8 < 64, even, odd)

    pl.semaphore_wait(barrier, len(peers))
    tcopy = remote(tsend, trecv, tsib_s, tsib_r, sibling)
    tcopy.start()

    tile = tirr_s[idx]
    prow = [[prod_s[i, j] for j in range(8)] for i in range(8)]
    ptile = [prod_s[i, tile] for i in range(8)]

    def factors():
        n = lax.broadcasted_iota(jnp.int32, (8, 512), 1)
        a_of, c_of = n // 8, lax.rem(n, 8)
        a_lane = lookup(a_of, [airr_s[a] for a in range(64)])
        c_lane = lookup(c_of, [cirr_s[c] for c in range(8)])
        a_rows = []
        for k in range(8):
            part = jnp.zeros((8, 128), jnp.int32)
            for i in range(8):
                part = jnp.where(rows8 == i, airr_s[k * 8 + i], part)
            a_rows.append(part)
        rank = jnp.zeros((8, 512), jnp.int32)
        for k in range(8):
            other = jnp.concatenate([a_rows[k]] * 4, axis=1)
            rank = rank + jnp.where(
                (other == a_lane) & (lax.broadcasted_iota(jnp.int32, (8, 512), 0) + k * 8 < a_of), 1, 0)
        rank = jnp.sum(rank, axis=0, keepdims=True) - round_s[0] * SLOTS
        block = lookup(lookup(a_lane, ptile) * 8 + c_lane, [e for row in prow for e in row])[0:1]
        code = jnp.where((rank >= 0) & (rank < SLOTS), block * 128 + c_of[0:1] * SLOTS + rank, -1)
        spot = lax.broadcasted_iota(jnp.int32, (128, 512), 0)
        for g in range(NIRR):
            pick = jnp.where(spot + g * 128 == code, 1.0, 0.0).astype(BF16)
            asel[g, :, :] = jnp.dot(pick, a_ref[...], preferred_element_type=F32).astype(BF16)

    def needs():
        need = lookup(lookup(pairs_ref[...], ptile), list(range(8))).astype(F32)
        eye = lax.broadcasted_iota(jnp.int32, (128, 128), 0) == lax.broadcasted_iota(jnp.int32, (128, 128), 1)
        for k in range(4):
            column = jnp.sum(jnp.where(eye, need[k:k + 1, :], 0.0), axis=1, keepdims=True)
            column = jnp.broadcast_to(column, (128, 128))
            for j in range(8):
                zz, yy = 2 * k + j // 4, j % 4
                rneed[pl.ds(yy * 128 + zz * 16, 16), :] = column[j * 16:(j + 1) * 16, :]

    def integrals(begin, end):
        def one(b, carry):
            for g in range(NIRR):
                main = fv[b, pl.ds(first[g], 6), :, :].reshape(WIN, 256)
                tail = fv[b, pl.ds(first[g] + 4, 2), :, :].reshape(64, 256)
                got = nt_dot(asel[g], jnp.concatenate([main, tail], axis=0))
                d_ref[g, :, pl.ds(pl.multiple_of(b * 16, 16), 16), :] = got.astype(BF16).reshape(8, 16, 256)
            return carry

        lax.fori_loop(begin, end, one, 0)

    lanes_a, lanes_b = pl.ds(0, CUT), pl.ds(CUT, KDIM - CUT)

    def unit(dz, dy, lanes):
        return g_ref.at[lax.rem(y + dy + 4, 4), lax.rem(z + dz + 8, 8), :, lanes]

    def group(dz, lanes):
        return g_ref.at[:, lax.rem(z + dz + 8, 8), :, lanes]

    away = (0, -1, 1, -2, 2, -3, 3, -4)

    def to_sibling(dz, lanes):
        slot = away.index(dz)
        return remote(group(dz, lanes), group(dz, lanes), sib_s.at[slot], sib_r.at[slot], sibling)

    def along_y(s):
        return remote(unit(0, 0, lanes_a), unit(0, 0, lanes_a), y_s.at[s - 1], y_r.at[s - 1], at_y(s))

    def along_y_in(s):
        return remote(unit(0, -s, lanes_a), unit(0, -s, lanes_a), y_s.at[s - 1], y_r.at[s - 1], at_y(s))

    def right(dz, s):
        return remote(group(dz, lanes_a), group(dz, lanes_a), rr_s.at[s], rr_r.at[s], at_z(1))

    def left(dz, s):
        return remote(group(dz, lanes_a), group(dz, lanes_a), rl_s.at[s], rl_r.at[s], at_z(-1))

    def along_z(s):
        return remote(unit(0, 0, lanes_b), unit(0, 0, lanes_b), zg_s.at[s - 1], zg_r.at[s - 1], at_z(s))

    def along_z_in(dz):
        s = (-dz) % 8
        return remote(unit(dz, 0, lanes_b), unit(dz, 0, lanes_b), zg_s.at[s - 1], zg_r.at[s - 1], at_z(s))

    def side(dz, dy):
        slot, way = away.index(dz), (dy + 1) // 2
        part = unit(dz, 0, lanes_b)
        return remote(part, part, side_s.at[slot, way], side_r.at[slot, way], at_y(dy))

    def side_in(dz, dy):
        slot, way = away.index(dz), (dy + 1) // 2
        part = unit(dz, -dy, lanes_b)
        return remote(part, part, side_s.at[slot, way], side_r.at[slot, way], at_y(dy))

    def onward(dz):
        slot, dy = away.index(dz), (1 if dz % 2 == 0 else -1)
        part = unit(dz, -dy, lanes_b)
        return remote(part, part, on_s.at[slot], on_r.at[slot], at_y(dy))

    def onward_in(dz):
        slot, dy = away.index(dz), (1 if dz % 2 == 0 else -1)
        part = unit(dz, 2, lanes_b)
        return remote(part, part, on_s.at[slot], on_r.at[slot], at_y(dy))

    def route_a(stage):
        if stage == 0:
            for s in range(1, 4):
                along_y(s).start()
            return
        if stage == 1:
            for s in range(1, 4):
                along_y_in(s).wait_recv()
            right(0, 0).start()
            left(0, 0).start()
            to_sibling(0, lanes_a).start()
            return
        if stage > 5:
            return
        right(1 - stage, stage - 2).wait_recv()
        if stage < 5:
            right(1 - stage, stage - 1).start()
            left(stage - 1, stage - 2).wait_recv()
            if stage < 4:
                left(stage - 1, stage - 1).start()
            to_sibling(1 - stage, lanes_a).start()
            to_sibling(stage - 1, lanes_a).start()
        else:
            to_sibling(-4, lanes_a).start()

    def both(far):
        return (-4,) if far == 4 else (0,) if far == 0 else (-far, far)

    def route_b(stage):
        if stage == 0:
            for s in (1, 7, 2, 6, 3, 5, 4):
                along_z(s).start()
        if stage <= 4:
            for dz in both(stage):
                if dz != 0:
                    along_z_in(dz).wait_recv()
                side(dz, 1).start()
                side(dz, -1).start()
        if 0 <= stage - 1 <= 4:
            for dz in both(stage - 1):
                side_in(dz, 1).wait_recv()
                side_in(dz, -1).wait_recv()
                onward(dz).start()
        if 0 <= stage - 2 <= 4:
            for dz in both(stage - 2):
                onward_in(dz).wait_recv()
                to_sibling(dz, lanes_b).start()

    def gather(stage):
        @pl.when(core == 0)
        def _():
            route_a(stage)

        @pl.when(core == 1)
        def _():
            route_b(stage)

    factors()
    tcopy.wait()
    own, other = tsend[...], trecv[...]
    @pl.when(core == 0)
    def _():
        g_ref[y, z, :, lanes_a] = jnp.concatenate([own[:, 0:CUT], other[:, 0:CUT]], axis=0).astype(BF16)

    @pl.when(core == 1)
    def _():
        g_ref[y, z, :, lanes_b] = jnp.concatenate([other[:, CUT:KDIM], own[:, CUT:KDIM]], axis=0).astype(BF16)

    gather(0)
    needs()
    for b in range(16):
        pltpu.make_async_copy(f_hbm.at[b], fv.at[b], fsem.at[b]).wait()
    done = 0
    for stage, until in ((1, 2), (2, 5), (3, 8), (4, 11), (5, 14), (6, 16)):
        integrals(done, until)
        done = until
        gather(stage)

    lane256 = lax.broadcasted_iota(jnp.int32, (256, 128), 1)
    for r in range(NIRR):
        blocks = [prod_s[prod_s[r, tile], cirr_s[c]] for c in range(8)]
        for c in range(8):
            rhs[r, :, c * 128:(c + 1) * 128] = d_ref[blocks[c], c, :, 0:128]
        for m in range(4):
            even = d_ref[blocks[2 * m], 2 * m, :, 128:256]
            odd = d_ref[blocks[2 * m + 1], 2 * m + 1, :, 128:256]
            rhs[r, :, 1024 + m * 128:1024 + (m + 1) * 128] = jnp.where(lane256 < 64, even, odd)

    @pl.when(core == 0)
    def _():
        for dz in away:
            to_sibling(dz, lanes_b).wait_recv()

    @pl.when(core == 1)
    def _():
        for dz in away:
            to_sibling(dz, lanes_a).wait_recv()

    def give(to, dx):
        other = lax.rem(con + dx, 4)
        return remote(
            xb.at[to, other], xr.at[y, dx], x_s.at[to, dx], x_r.at[y, dx], ((z * 4 + to) * 2 + core, other))

    def given(src, dx):
        return remote(xb.at[src, con], xr.at[src, dx], x_s.at[src, dx], x_r.at[src, dx], at_x(dx))

    for h in range(2):
        rows = pl.ds(h * 256, 256)
        left_side = g_ref[2 * h:2 * h + 2].reshape(256, KDIM)
        for r in range(NIRR):
            got = nt_dot(left_side, rhs[r])
            for k in range(2):
                part = got[:, k * 128:(k + 1) * 128]
                acc[k, rows, :] = part if r == 0 else jnp.where(rneed[rows, :] == float(r), part, acc[k, rows, :])
        for j in range(2):
            to = 2 * h + j
            for r in range(4):
                for q in range(4):
                    for k in range(2):
                        xf[pl.ds(r * 64 + q * 2 + k, 8, stride=8), :] = acc[
                            k, pl.ds(to * 128 + (q // 2) * 8 + r * 2 + q % 2, 8, stride=16), :]
            xb[to, :, :, :] = xf[...].astype(BF16).reshape(4, 64, 128)
            for dx in range(1, 4):
                give(to, dx).start()

            @pl.when(y != to)
            def _():
                give(to, 0).start()

    xr[y, 0, :, :] = xb[y, con, :, :]
    for src in range(4):
        @pl.when(y != src)
        def _():
            given(src, 0).wait_recv()

        for dx in range(1, 4):
            given(src, dx).wait_recv()
        total = (xr[src, 0].astype(F32) + xr[src, 1].astype(F32)) + (xr[src, 2].astype(F32) + xr[src, 3].astype(F32))
        for zz in range(8):
            for k in range(2):
                zf[zz, k, src * 4:(src + 1) * 4, :] = total[zz * 8 + k * 4:zz * 8 + k * 4 + 4, :]
    zb[...] = zf[...].astype(BF16)

    def own_z(s, flip):
        to = lax.rem(z + s, 8)
        kk = 1 - core if flip else core
        return remote(
            zb.at[to, kk], vb.at[core, z], ze_s.at[s, flip], ze_r.at[s, flip], ((to * 4 + y) * 2 + kk, con))

    def own_z_in(s, flip):
        src = lax.rem(z + 8 - s, 8)
        kk = 1 - core if flip else core
        return remote(
            zb.at[src, kk], vb.at[kk, src], ze_s.at[s, flip], ze_r.at[s, flip], ((src * 4 + y) * 2 + kk, con))

    routes = [(s, flip) for s in (4, 3, 5, 2, 6, 1, 7, 0) for flip in (0, 1) if (s, flip) != (0, 0)]
    for s, flip in routes:
        own_z(s, flip).start()
    vb[core, z, :, :] = zb[z, core, :, :]
    for s, flip in routes:
        own_z_in(s, flip).wait_recv()
    out_ref[...] = vb[...]

    @pl.when(core == 0)
    def _():
        for s in range(1, 4):
            along_y(s).wait_send()
        for s in range(4):
            right(-s, s).wait_send()
        for s in range(3):
            left(s, s).wait_send()
        for dz in away:
            to_sibling(dz, lanes_a).wait_send()

    @pl.when(core == 1)
    def _():
        for s in range(1, 8):
            along_z(s).wait_send()
        for dz in away:
            side(dz, 1).wait_send()
            side(dz, -1).wait_send()
            onward(dz).wait_send()
            to_sibling(dz, lanes_b).wait_send()

    for to in range(4):
        for dx in range(1, 4):
            give(to, dx).wait_send()

        @pl.when(y != to)
        def _():
            give(to, 0).wait_send()

    for s, flip in routes:
        own_z(s, flip).wait_send()


def place_kernel(
    pair_s, prod_s, round_s, airr_ref, tlen_ref, tirr_ref, v_ref, prev_ref, out_ref, rounds_s, v32, left, expand, *, first_round
):
    idx = lax.axis_index("idx")
    con = lax.axis_index("con")
    lane16 = lax.broadcasted_iota(jnp.int32, (16, 128), 1)
    v32[...] = v_ref[...].reshape(2, 128, 128).astype(F32)
    for h in range(2):
        parts = []
        for pp in range(2):
            for kappa in range(2):
                parts.append(v32[kappa, pl.ds(pp * 2 + h, 32, stride=4), :])
        turned = jnp.concatenate(parts, axis=0).T
        for bl in range(8):
            piece = turned[bl * 16:(bl + 1) * 16, :]
            for pp in range(2):
                kept = jnp.where((lane16 // 64) == pp, piece, 0.0)
                left[pl.ds(pp * 16, 16), (h * 8 + bl) * 128:(h * 8 + bl + 1) * 128] = kept
    source = lax.broadcasted_iota(jnp.int32, (128, 1024), 0)
    lane = lax.broadcasted_iota(jnp.int32, (128, 1024), 1)
    local = lax.rem(source, 64)
    tile_first = (lax.rem(local, 32) * 2 + local // 32) * 16
    for b in range(16):
        expand[b * 128:(b + 1) * 128, :] = jnp.where(tile_first + b == lane, 1.0, 0.0).astype(BF16)
    a_row = airr_ref[...]
    row = lax.broadcasted_iota(jnp.int32, (64, 64), 0)
    col = lax.broadcasted_iota(jnp.int32, (64, 64), 1)
    a_col = jnp.sum(jnp.where(row == col, a_row, 0), axis=1, keepdims=True)
    rank = jnp.sum(jnp.where((a_col == a_row) & (col < row), 1, 0), axis=1, keepdims=True)
    rounds_s[0] = jnp.max(rank) // SLOTS + 1
    rank = rank - round_s[0] * SLOTS
    slot = lax.broadcasted_iota(jnp.int32, (64, 32), 1)
    full = left[...].astype(BF16)
    held = (rank >= 0) & (rank < SLOTS)
    pick = [jnp.where(held & (slot == rank + pp * 16), 1.0, 0.0) for pp in range(2)]
    pick = jnp.concatenate(pick, axis=0).astype(BF16)
    chosen = jnp.dot(pick, full, preferred_element_type=F32).astype(BF16)
    values = jnp.dot(chosen, expand[...], preferred_element_type=F32)
    spread = jnp.where(
        lax.broadcasted_iota(jnp.int32, (64, 1024), 0) == lax.broadcasted_iota(jnp.int32, (64, 1024), 1) // 16, 1.0, 0.0
    ).astype(BF16)

    def lanes_of(ref):
        wide = jnp.broadcast_to(ref[...], (8, 64)).astype(F32).astype(BF16)
        return jnp.dot(wide, spread, preferred_element_type=F32)[0:1]

    length, irrep = lanes_of(tlen_ref), lanes_of(tirr_ref).astype(jnp.int32)
    live = lax.rem(lax.broadcasted_iota(jnp.int32, (1, 1024), 1), 16).astype(F32) < length
    for pp in range(2):
        pair_irr = pair_s[idx * 8 + con * 2 + pp]
        need = lookup(irrep, [prod_s[pair_irr, i] for i in range(8)])
        need = jnp.where(live, need, -1)
        keep = a_col == need
        got = jnp.where(keep, values[pp * 64:(pp + 1) * 64, :], 0.0)
        if not first_round:
            got = got + prev_ref[pp, :, :]
        out_ref[pp, :, :] = got


def smem():
    return pl.BlockSpec(memory_space=pltpu.SMEM)


def vmem():
    return pl.BlockSpec(memory_space=pltpu.VMEM)


def ladder(pair_irrep, a_irrep, c_irrep, irrep_start, product, tile_irrep, number, amplitude, fit, pairs, fitting):
    dma = pltpu.SemaphoreType.DMA
    return pl.pallas_call(
        ladder_kernel,
        out_shape=jax.ShapeDtypeStruct((2, 8, 16, 128), BF16),
        in_specs=[smem()] * 7 + [vmem()] * 3 + [pl.BlockSpec(memory_space=pltpu.HBM)],
        out_specs=vmem(),
        scratch_shapes=[
            pltpu.VMEM((16, 25, 32, 256), BF16),
            pltpu.VMEM((64, 896), F32),
            pltpu.VMEM((2, 64, 128), F32),
            pltpu.VMEM((8, KDIM), F32),
            pltpu.VMEM((8, KDIM), F32),
            pltpu.VMEM((4, 8, 16, KDIM), BF16),
            pltpu.VMEM((NIRR, 128, 256), BF16),
            pltpu.VMEM((NIRR, 8, 256, 256), BF16),
            pltpu.VMEM((NIRR, 256, KDIM), BF16),
            pltpu.VMEM((512, 128), F32),
            pltpu.VMEM((2, 512, 128), F32),
            pltpu.VMEM((256, 128), F32),
            pltpu.VMEM((4, 4, 64, 128), BF16),
            pltpu.VMEM((4, 4, 64, 128), BF16),
            pltpu.VMEM((8, 2, 16, 128), F32),
            pltpu.VMEM((8, 2, 16, 128), BF16),
            pltpu.VMEM((2, 8, 16, 128), BF16),
            dma((16,)), dma, dma, dma((3,)), dma((3,)), dma((4,)), dma((4,)), dma((3,)), dma((3,)),
            dma((8,)), dma((8,)), dma((7,)), dma((7,)), dma((8, 2)), dma((8, 2)), dma((8,)), dma((8,)),
            dma((4, 4)), dma((4, 4)), dma((8, 2)), dma((8, 2)),
        ],
        compiler_params=pltpu.CompilerParams(
            collective_id=0, has_side_effects=True, vmem_limit_bytes=48 * 1024 * 1024),
        name="ladder",
    )(pair_irrep, a_irrep, c_irrep, irrep_start, product, tile_irrep, number, amplitude, fit, pairs, fitting)


def place(pair_irrep, product, number, a_irrep, tile_len, tile_irrep, gathered, previous, first_round):
    return pl.pallas_call(
        functools.partial(place_kernel, first_round=first_round),
        out_shape=(jax.ShapeDtypeStruct((2, 64, 1024), F32), jax.ShapeDtypeStruct((1,), jnp.int32)),
        in_specs=[smem()] * 3 + [vmem()] * 5,
        out_specs=(vmem(), smem()),
        scratch_shapes=[pltpu.VMEM((2, 128, 128), F32), pltpu.VMEM((32, 2048), F32), pltpu.VMEM((2048, 1024), BF16)],
        compiler_params=pltpu.CompilerParams(vmem_limit_bytes=48 * 1024 * 1024),
        name="place" if first_round else "place_more",
    )(pair_irrep, product, number, a_irrep, tile_len, tile_irrep, gathered, previous)


def body(
    amplitude, pair_irrep, fit_ac, fitting_tensor_bd, a_irrep, c_irrep, irrep_start, product, tile_len, tile_irrep
):
    fitting = jnp.transpose(fitting_tensor_bd, (1, 2, 0)).reshape(16, 25, 32, 256)
    fit = jnp.transpose(fit_ac, (1, 2, 0)).reshape(512, 256)
    pairs = pair_irrep.reshape(4, 128)
    a_row, len_row, irr_row = a_irrep.reshape(1, 64), tile_len.reshape(1, 64), tile_irrep.reshape(1, 64)
    def one_round(number, previous, first_round):
        number = jnp.asarray(number, jnp.int32).reshape(1)
        gathered = ladder(
            pair_irrep, a_irrep, c_irrep, irrep_start, product, tile_irrep, number, amplitude, fit, pairs, fitting)
        return place(pair_irrep, product, number, a_row, len_row, irr_row, gathered, previous, first_round)

    out, rounds = one_round(0, jnp.zeros((2, 64, 1024), F32), False)

    def more(carry):
        return carry[0] < rounds[0]

    def step(carry):
        number, out = carry
        return number + 1, one_round(number, out, False)[0]

    return lax.while_loop(more, step, (jnp.int32(1), out))[1]


def solution(mesh):
    placed = (
        P("idx", None, None),
        P(),
        P("con", None, None),
        P("con", "idx", None),
        P(),
        P(),
        P(),
        P(),
        P(),
        P(),
    )
    return jax.shard_map(
        body, mesh=mesh, in_specs=placed, out_specs=P(("idx", "con"), None, None), check_vma=False
    )
```

```python
import functools

import jax
import jax.numpy as jnp
from jax import lax
from jax.experimental import pallas as pl
from jax.experimental.pallas import tpu as pltpu
from jax.sharding import PartitionSpec as P

MESH = pl.DeviceIdType.MESH
BW = 16
NIRR = 8
WIN = 192
SLOTS = 16
NV = 800
KDIM = 8 * WIN
CUT = 256
F32 = jnp.float32
BF16 = jnp.bfloat16


def nt_dot(left, right):
    return lax.dot_general(left, right, (((1,), (1,)), ((), ())), preferred_element_type=F32)


def lookup(index, entries):
    out = jnp.zeros_like(index)
    for spot, entry in enumerate(entries):
        out = jnp.where(index == spot, entry, out)
    return out


def ladder_kernel(
    pair_s, airr_s, cirr_s, start_s, prod_s, tirr_s, round_s,
    amp_ref, a_ref, pairs_ref, f_hbm,
    out_ref,
    fv, x32, tc, tsend, trecv, ga, gb, asel, d_ref, rhs, rneed, acc, xf, xb, xr, zf, zb, vb,
    fsem, tsib_s, tsib_r, y_s, y_r, gz_s, gz_r, sib_s, sib_r, one_s, one_r, zg_s, zg_r, side_s, side_r, on_s, on_r,
    x_s, x_r, ze_s, ze_r,
):
    idx = lax.axis_index("idx")
    con = lax.axis_index("con")
    core = lax.rem(idx, 2)
    chip = idx // 2
    y = lax.rem(chip, 4)
    z = chip // 4
    sibling = (chip * 2 + 1 - core, con)

    def at_y(dy):
        return ((z * 4 + lax.rem(y + dy + 4, 4)) * 2 + core, con)

    def at_z(dz):
        return ((lax.rem(z + dz + 8, 8) * 4 + y) * 2 + core, con)

    def at_x(dx):
        return (idx, lax.rem(con + dx, 4))

    def remote(src, dst, send, recv, to):
        return pltpu.make_async_remote_copy(
            src_ref=src, dst_ref=dst, send_sem=send, recv_sem=recv, device_id=to, device_id_type=MESH)

    for b in range(16):
        pltpu.make_async_copy(f_hbm.at[b], fv.at[b], fsem.at[b]).start()

    barrier = pltpu.get_barrier_semaphore()
    peers = [sibling]
    for s in range(1, 8):
        there = lax.rem(z + s, 8) * 4 + y
        peers += [(there * 2 + core, con), (there * 2 + 1 - core, con)]
    for s in range(4):
        for dx in range(4):
            if s or dx:
                peers.append(((z * 4 + lax.rem(y + s, 4)) * 2 + core, lax.rem(con + dx, 4)))
    for peer in peers:
        pl.semaphore_signal(barrier, inc=1, device_id=peer, device_id_type=MESH)

    first = [jnp.minimum(start_s[g] // 32, (NV - WIN) // 32) for g in range(NIRR)]
    base = [first[g] * 32 for g in range(NIRR)]
    low = [start_s[g] - base[g] for g in range(NIRR)]
    high = [(start_s[g + 1] if g < 7 else NV) - base[g] for g in range(NIRR)]
    x32[:, 768:896] = jnp.zeros((64, 128), F32)
    x32[:, 0:NV] = amp_ref[...].astype(F32).reshape(64, NV)
    rows8 = lax.broadcasted_iota(jnp.int32, (8, 128), 0)
    target = []
    for p in range(8):
        irr = pair_s[idx * 8 + p]
        part = jnp.zeros((8, 128), jnp.int32)
        for c in range(8):
            part = jnp.where(rows8 == c, prod_s[irr, cirr_s[c]], part)
        target.append(part)
    target = jnp.concatenate(target, axis=0)
    target = jnp.concatenate([target, target], axis=1)
    lanes = lax.broadcasted_iota(jnp.int32, (64, 256), 1)
    window = jnp.zeros((64, 256), F32)
    whole = x32[...]
    for g in range(NIRR):
        moved = pltpu.roll(whole, 896 - base[g], 1)[:, 0:256]
        window = jnp.where((target == g) & (lanes >= low[g]) & (lanes < high[g]), moved, window)
    tc[0, :, :] = window[:, 0:128]
    tc[1, :, :] = window[:, 128:256]
    lane8 = lax.broadcasted_iota(jnp.int32, (8, 128), 1)
    for c in range(8):
        tsend[:, c * 128:(c + 1) * 128] = tc[0, pl.ds(c, 8, stride=8), :]
    for m in range(4):
        even = tc[1, pl.ds(2 * m, 8, stride=8), :]
        odd = pltpu.roll(tc[1, pl.ds(2 * m + 1, 8, stride=8), :], 64, 1)
        tsend[:, 1024 + m * 128:1024 + (m + 1) * 128] = jnp.where(lane8 < 64, even, odd)

    pl.semaphore_wait(barrier, len(peers))
    tcopy = remote(tsend, trecv, tsib_s, tsib_r, sibling)
    tcopy.start()

    tile = tirr_s[idx]
    prow = [[prod_s[i, j] for j in range(8)] for i in range(8)]
    ptile = [prod_s[i, tile] for i in range(8)]

    def factors():
        n = lax.broadcasted_iota(jnp.int32, (8, 512), 1)
        a_of, c_of = n // 8, lax.rem(n, 8)
        a_lane = lookup(a_of, [airr_s[a] for a in range(64)])
        c_lane = lookup(c_of, [cirr_s[c] for c in range(8)])
        a_rows = []
        for k in range(8):
            part = jnp.zeros((8, 128), jnp.int32)
            for i in range(8):
                part = jnp.where(rows8 == i, airr_s[k * 8 + i], part)
            a_rows.append(part)
        rank = jnp.zeros((8, 512), jnp.int32)
        for k in range(8):
            other = jnp.concatenate([a_rows[k]] * 4, axis=1)
            rank = rank + jnp.where(
                (other == a_lane) & (lax.broadcasted_iota(jnp.int32, (8, 512), 0) + k * 8 < a_of), 1, 0)
        rank = jnp.sum(rank, axis=0, keepdims=True) - round_s[0] * SLOTS
        block = lookup(lookup(a_lane, ptile) * 8 + c_lane, [e for row in prow for e in row])[0:1]
        code = jnp.where((rank >= 0) & (rank < SLOTS), block * 128 + c_of[0:1] * SLOTS + rank, -1)
        spot = lax.broadcasted_iota(jnp.int32, (128, 512), 0)
        for g in range(NIRR):
            pick = jnp.where(spot + g * 128 == code, 1.0, 0.0).astype(BF16)
            asel[g, :, :] = jnp.dot(pick, a_ref[...], preferred_element_type=F32).astype(BF16)

    def needs():
        need = lookup(lookup(pairs_ref[...], ptile), list(range(8))).astype(F32)
        eye = lax.broadcasted_iota(jnp.int32, (128, 128), 0) == lax.broadcasted_iota(jnp.int32, (128, 128), 1)
        for k in range(4):
            column = jnp.sum(jnp.where(eye, need[k:k + 1, :], 0.0), axis=1, keepdims=True)
            column = jnp.broadcast_to(column, (128, 128))
            rneed[2 * k, :, :] = column[0:64, :]
            rneed[2 * k + 1, :, :] = column[64:128, :]

    def integrals(begin, end):
        def one(b, carry):
            for g in range(NIRR):
                main = fv[b, pl.ds(first[g], 6), :, :].reshape(WIN, 256)
                tail = fv[b, pl.ds(first[g] + 4, 2), :, :].reshape(64, 256)
                got = nt_dot(asel[g], jnp.concatenate([main, tail], axis=0))
                d_ref[g, :, pl.ds(pl.multiple_of(b * 16, 16), 16), :] = got.astype(BF16).reshape(8, 16, 256)
            return carry

        lax.fori_loop(begin, end, one, 0)

    def unit_a(dy):
        return ga.at[z, lax.rem(y + dy + 4, 4)]

    def group_a(dz):
        return ga.at[lax.rem(z + dz + 8, 8)]

    def unit(dz, dy):
        return gb.at[lax.rem(y + dy + 4, 4), lax.rem(z + dz + 8, 8)]

    away = (0, -1, 1, -2, 2, -3, 3, -4)

    def to_sibling(dz):
        slot = away.index(dz)
        return remote(group_a(dz), group_a(dz), sib_s.at[slot], sib_r.at[slot], sibling)

    def unit_to_sibling(dz, dy):
        slot, part = away.index(dz), unit(dz, dy)
        return remote(part, part, one_s.at[slot, dy % 4], one_r.at[slot, dy % 4], sibling)

    def along_y(s):
        return remote(unit_a(0), unit_a(0), y_s.at[s - 1], y_r.at[s - 1], at_y(s))

    def along_y_in(s):
        return remote(unit_a(-s), unit_a(-s), y_s.at[s - 1], y_r.at[s - 1], at_y(s))

    def groups_z(s):
        return remote(group_a(0), group_a(0), gz_s.at[s - 1], gz_r.at[s - 1], at_z(s))

    def groups_z_in(dz):
        s = (-dz) % 8
        return remote(group_a(dz), group_a(dz), gz_s.at[s - 1], gz_r.at[s - 1], at_z(s))

    def along_z(s):
        return remote(unit(0, 0), unit(0, 0), zg_s.at[s - 1], zg_r.at[s - 1], at_z(s))

    def along_z_in(dz):
        s = (-dz) % 8
        return remote(unit(dz, 0), unit(dz, 0), zg_s.at[s - 1], zg_r.at[s - 1], at_z(s))

    def side(dz, dy):
        slot, way = away.index(dz), (dy + 1) // 2
        part = unit(dz, 0)
        return remote(part, part, side_s.at[slot, way], side_r.at[slot, way], at_y(dy))

    def side_in(dz, dy):
        slot, way = away.index(dz), (dy + 1) // 2
        part = unit(dz, -dy)
        return remote(part, part, side_s.at[slot, way], side_r.at[slot, way], at_y(dy))

    def onward(dz):
        slot, dy = away.index(dz), (1 if dz % 2 == 0 else -1)
        part = unit(dz, -dy)
        return remote(part, part, on_s.at[slot], on_r.at[slot], at_y(dy))

    def onward_in(dz):
        slot, dy = away.index(dz), (1 if dz % 2 == 0 else -1)
        part = unit(dz, 2)
        return remote(part, part, on_s.at[slot], on_r.at[slot], at_y(dy))

    def route_a(stage):
        if stage == 0:
            for s in range(1, 4):
                along_y(s).start()
            return
        if stage == 1:
            for s in range(1, 4):
                along_y_in(s).wait_recv()
            for s in (1, 7, 2, 6, 3, 5, 4):
                groups_z(s).start()
            to_sibling(0).start()
            return
        if stage > 5:
            return
        for dz in both(stage - 1):
            groups_z_in(dz).wait_recv()
            to_sibling(dz).start()

    def both(far):
        return (-4,) if far == 4 else (0,) if far == 0 else (-far, far)

    def route_b(stage):
        arrive = {1: (-1, 1), 2: (-2, 2), 3: (-3, 3, -4)}
        pass_on = {1: (0,), 3: (-1, 1), 4: (-2, 2), 5: (-3, 3, -4)}
        take = {4: (0, -1, 1), 5: (-2, 2), 6: (-3, 3, -4)}
        if stage == 0:
            for s in (7, 1, 6, 2, 5, 3, 4):
                along_z(s).start()
            side(0, 1).start()
            side(0, -1).start()
            unit_to_sibling(0, 0).start()
        for dz in arrive.get(stage, ()):
            along_z_in(dz).wait_recv()
            side(dz, 1).start()
            side(dz, -1).start()
            unit_to_sibling(dz, 0).start()
        for dz in pass_on.get(stage, ()):
            dy = 1 if dz % 2 == 0 else -1
            side_in(dz, dy).wait_recv()
            onward(dz).start()
            unit_to_sibling(dz, -dy).start()
            side_in(dz, -dy).wait_recv()
            unit_to_sibling(dz, dy).start()
        for dz in take.get(stage, ()):
            onward_in(dz).wait_recv()
            unit_to_sibling(dz, 2).start()

    def gather(stage):
        @pl.when(core == 0)
        def _():
            route_a(stage)

        @pl.when(core == 1)
        def _():
            route_b(stage)

    factors()
    tcopy.wait()
    own, other = tsend[...], trecv[...]
    @pl.when(core == 0)
    def _():
        ga[z, y, :, :] = jnp.concatenate([own[:, 0:CUT], other[:, 0:CUT]], axis=0).astype(BF16)

    @pl.when(core == 1)
    def _():
        gb[y, z, :, :] = jnp.concatenate([other[:, CUT:KDIM], own[:, CUT:KDIM]], axis=0).astype(BF16)

    gather(0)
    needs()
    for b in range(16):
        pltpu.make_async_copy(f_hbm.at[b], fv.at[b], fsem.at[b]).wait()
    done = 0
    for stage, until in ((1, 3), (2, 6), (3, 9), (4, 13), (5, 16)):
        integrals(done, until)
        done = until
        gather(stage)

    lane256 = lax.broadcasted_iota(jnp.int32, (256, 128), 1)
    for r in range(NIRR):
        blocks = [prod_s[prod_s[r, tile], cirr_s[c]] for c in range(8)]
        for c in range(8):
            rhs[r, :, c * 128:(c + 1) * 128] = d_ref[blocks[c], c, :, 0:128]
        for m in range(4):
            even = d_ref[blocks[2 * m], 2 * m, :, 128:256]
            odd = d_ref[blocks[2 * m + 1], 2 * m + 1, :, 128:256]
            rhs[r, :, 1024 + m * 128:1024 + (m + 1) * 128] = jnp.where(lane256 < 64, even, odd)

    def from_sibling(part):
        @pl.when(core == 0)
        def _():
            for dz in part:
                for dy in range(4):
                    unit_to_sibling(dz, dy).wait_recv()

        @pl.when(core == 1)
        def _():
            for dz in part:
                to_sibling(dz).wait_recv()

    def give(h, to, dx):
        other = lax.rem(con + dx, 4)
        return remote(
            xb.at[h, to, other], xr.at[h, y, dx], x_s.at[h, to, dx], x_r.at[h, y, dx],
            ((z * 4 + to) * 2 + core, other))

    def given(h, src, dx):
        return remote(
            xb.at[h, src, con], xr.at[h, src, dx], x_s.at[h, src, dx], x_r.at[h, src, dx],
            ((z * 4 + src) * 2 + core, lax.rem(con + dx, 4)))

    parts = (away[0:4], away[4:8])
    for h in range(2):
        if h == 1:
            gather(6)
        from_sibling(parts[h])
        places = [lax.rem(z + dz + 8, 8) for dz in parts[h]]
        left_side = jnp.concatenate(
            [jnp.concatenate([ga[zz].reshape(64, CUT) for zz in places], axis=0),
             jnp.concatenate([gb[:, zz, :, :].reshape(64, KDIM - CUT) for zz in places], axis=0)], axis=1)
        need = jnp.concatenate([rneed[zz, :, :] for zz in places], axis=0)
        for r in range(NIRR):
            got = nt_dot(left_side, rhs[r])
            for k in range(2):
                part = got[:, k * 128:(k + 1) * 128]
                acc[k, :, :] = part if r == 0 else jnp.where(need == float(r), part, acc[k, :, :])
        for to in range(4):
            for r in range(4):
                for q in range(4):
                    for k in range(2):
                        xf[pl.ds(r * 32 + q * 2 + k, 4, stride=8), :] = acc[
                            k, pl.ds(to * 16 + (q // 2) * 8 + r * 2 + q % 2, 4, stride=64), :]
            xb[h, to, :, :, :] = xf[...].astype(BF16).reshape(4, 32, 128)
            for dx in range(1, 4):
                give(h, to, dx).start()

            @pl.when(y != to)
            def _():
                give(h, to, 0).start()

        xr[h, y, 0, :, :] = xb[h, y, con, :, :]

    def own_z(dz, flip):
        to = lax.rem(z + dz + 8, 8)
        kk = 1 - core if flip else core
        return remote(
            zb.at[to, kk], vb.at[core, z], ze_s.at[dz % 8, flip], ze_r.at[dz % 8, flip],
            ((to * 4 + y) * 2 + kk, con))

    def own_z_in(dz, flip):
        src = lax.rem(z + 8 - dz, 8)
        kk = 1 - core if flip else core
        return remote(
            zb.at[src, kk], vb.at[kk, src], ze_s.at[dz % 8, flip], ze_r.at[dz % 8, flip],
            ((src * 4 + y) * 2 + kk, con))

    routes = [(dz, flip) for dz in away for flip in (0, 1) if (dz, flip) != (0, 0)]
    for h in range(2):
        places = [lax.rem(z + dz + 8, 8) for dz in parts[h]]
        for src in range(4):
            @pl.when(y != src)
            def _():
                given(h, src, 0).wait_recv()

            for dx in range(1, 4):
                given(h, src, dx).wait_recv()
            total = (xr[h, src, 0].astype(F32) + xr[h, src, 1].astype(F32)) + (
                xr[h, src, 2].astype(F32) + xr[h, src, 3].astype(F32))
            for i in range(4):
                for k in range(2):
                    zf[i, k, src * 4:(src + 1) * 4, :] = total[i * 8 + k * 4:i * 8 + k * 4 + 4, :]
        for i in range(4):
            zb[places[i], :, :, :] = zf[i, :, :, :].astype(BF16)
        for dz, flip in routes:
            if dz in parts[h]:
                own_z(dz, flip).start()
    vb[core, z, :, :] = zb[z, core, :, :]
    for dz, flip in routes:
        own_z_in(dz, flip).wait_recv()
    out_ref[...] = vb[...]

    @pl.when(core == 0)
    def _():
        for s in range(1, 4):
            along_y(s).wait_send()
        for s in range(1, 8):
            groups_z(s).wait_send()
        for dz in away:
            to_sibling(dz).wait_send()

    @pl.when(core == 1)
    def _():
        for s in range(1, 8):
            along_z(s).wait_send()
        for dz in away:
            side(dz, 1).wait_send()
            side(dz, -1).wait_send()
            onward(dz).wait_send()
            for dy in range(4):
                unit_to_sibling(dz, dy).wait_send()

    for h in range(2):
        for to in range(4):
            for dx in range(1, 4):
                give(h, to, dx).wait_send()

            @pl.when(y != to)
            def _():
                give(h, to, 0).wait_send()

    for dz, flip in routes:
        own_z(dz, flip).wait_send()


def place_kernel(
    pair_s, prod_s, round_s, airr_ref, tlen_ref, tirr_ref, v_ref, prev_ref, out_ref, rounds_s, v32, left, expand, *, first_round
):
    idx = lax.axis_index("idx")
    con = lax.axis_index("con")
    lane16 = lax.broadcasted_iota(jnp.int32, (16, 128), 1)
    v32[...] = v_ref[...].reshape(2, 128, 128).astype(F32)
    for h in range(2):
        parts = []
        for pp in range(2):
            for kappa in range(2):
                parts.append(v32[kappa, pl.ds(pp * 2 + h, 32, stride=4), :])
        turned = jnp.concatenate(parts, axis=0).T
        for bl in range(8):
            piece = turned[bl * 16:(bl + 1) * 16, :]
            for pp in range(2):
                kept = jnp.where((lane16 // 64) == pp, piece, 0.0)
                left[pl.ds(pp * 16, 16), (h * 8 + bl) * 128:(h * 8 + bl + 1) * 128] = kept
    source = lax.broadcasted_iota(jnp.int32, (128, 1024), 0)
    lane = lax.broadcasted_iota(jnp.int32, (128, 1024), 1)
    local = lax.rem(source, 64)
    tile_first = (lax.rem(local, 32) * 2 + local // 32) * 16
    for b in range(16):
        expand[b * 128:(b + 1) * 128, :] = jnp.where(tile_first + b == lane, 1.0, 0.0).astype(BF16)
    a_row = airr_ref[...]
    row = lax.broadcasted_iota(jnp.int32, (64, 64), 0)
    col = lax.broadcasted_iota(jnp.int32, (64, 64), 1)
    a_col = jnp.sum(jnp.where(row == col, a_row, 0), axis=1, keepdims=True)
    rank = jnp.sum(jnp.where((a_col == a_row) & (col < row), 1, 0), axis=1, keepdims=True)
    rounds_s[0] = jnp.max(rank) // SLOTS + 1
    rank = rank - round_s[0] * SLOTS
    slot = lax.broadcasted_iota(jnp.int32, (64, 32), 1)
    full = left[...].astype(BF16)
    held = (rank >= 0) & (rank < SLOTS)
    pick = [jnp.where(held & (slot == rank + pp * 16), 1.0, 0.0) for pp in range(2)]
    pick = jnp.concatenate(pick, axis=0).astype(BF16)
    chosen = jnp.dot(pick, full, preferred_element_type=F32).astype(BF16)
    values = jnp.dot(chosen, expand[...], preferred_element_type=F32)
    spread = jnp.where(
        lax.broadcasted_iota(jnp.int32, (64, 1024), 0) == lax.broadcasted_iota(jnp.int32, (64, 1024), 1) // 16, 1.0, 0.0
    ).astype(BF16)

    def lanes_of(ref):
        wide = jnp.broadcast_to(ref[...], (8, 64)).astype(F32).astype(BF16)
        return jnp.dot(wide, spread, preferred_element_type=F32)[0:1]

    length, irrep = lanes_of(tlen_ref), lanes_of(tirr_ref).astype(jnp.int32)
    live = lax.rem(lax.broadcasted_iota(jnp.int32, (1, 1024), 1), 16).astype(F32) < length
    for pp in range(2):
        pair_irr = pair_s[idx * 8 + con * 2 + pp]
        need = lookup(irrep, [prod_s[pair_irr, i] for i in range(8)])
        need = jnp.where(live, need, -1)
        keep = a_col == need
        got = jnp.where(keep, values[pp * 64:(pp + 1) * 64, :], 0.0)
        if not first_round:
            got = got + prev_ref[pp, :, :]
        out_ref[pp, :, :] = got


def smem():
    return pl.BlockSpec(memory_space=pltpu.SMEM)


def vmem():
    return pl.BlockSpec(memory_space=pltpu.VMEM)


def ladder(pair_irrep, a_irrep, c_irrep, irrep_start, product, tile_irrep, number, amplitude, fit, pairs, fitting):
    dma = pltpu.SemaphoreType.DMA
    return pl.pallas_call(
        ladder_kernel,
        out_shape=jax.ShapeDtypeStruct((2, 8, 16, 128), BF16),
        in_specs=[smem()] * 7 + [vmem()] * 3 + [pl.BlockSpec(memory_space=pltpu.HBM)],
        out_specs=vmem(),
        scratch_shapes=[
            pltpu.VMEM((16, 25, 32, 256), BF16),
            pltpu.VMEM((64, 896), F32),
            pltpu.VMEM((2, 64, 128), F32),
            pltpu.VMEM((8, KDIM), F32),
            pltpu.VMEM((8, KDIM), F32),
            pltpu.VMEM((8, 4, 16, CUT), BF16),
            pltpu.VMEM((4, 8, 16, KDIM - CUT), BF16),
            pltpu.VMEM((NIRR, 128, 256), BF16),
            pltpu.VMEM((NIRR, 8, 256, 256), BF16),
            pltpu.VMEM((NIRR, 256, KDIM), BF16),
            pltpu.VMEM((8, 64, 128), F32),
            pltpu.VMEM((2, 256, 128), F32),
            pltpu.VMEM((128, 128), F32),
            pltpu.VMEM((2, 4, 4, 32, 128), BF16),
            pltpu.VMEM((2, 4, 4, 32, 128), BF16),
            pltpu.VMEM((4, 2, 16, 128), F32),
            pltpu.VMEM((8, 2, 16, 128), BF16),
            pltpu.VMEM((2, 8, 16, 128), BF16),
            dma((16,)), dma, dma, dma((3,)), dma((3,)), dma((7,)), dma((7,)),
            dma((8,)), dma((8,)), dma((8, 4)), dma((8, 4)), dma((7,)), dma((7,)), dma((8, 2)), dma((8, 2)), dma((8,)), dma((8,)),
            dma((2, 4, 4)), dma((2, 4, 4)), dma((8, 2)), dma((8, 2)),
        ],
        compiler_params=pltpu.CompilerParams(
            collective_id=0, has_side_effects=True, vmem_limit_bytes=48 * 1024 * 1024),
        name="ladder",
    )(pair_irrep, a_irrep, c_irrep, irrep_start, product, tile_irrep, number, amplitude, fit, pairs, fitting)


def place(pair_irrep, product, number, a_irrep, tile_len, tile_irrep, gathered, previous, first_round):
    return pl.pallas_call(
        functools.partial(place_kernel, first_round=first_round),
        out_shape=(jax.ShapeDtypeStruct((2, 64, 1024), F32), jax.ShapeDtypeStruct((1,), jnp.int32)),
        in_specs=[smem()] * 3 + [vmem()] * 5,
        out_specs=(vmem(), smem()),
        scratch_shapes=[pltpu.VMEM((2, 128, 128), F32), pltpu.VMEM((32, 2048), F32), pltpu.VMEM((2048, 1024), BF16)],
        compiler_params=pltpu.CompilerParams(vmem_limit_bytes=48 * 1024 * 1024),
        name="place" if first_round else "place_more",
    )(pair_irrep, product, number, a_irrep, tile_len, tile_irrep, gathered, previous)


def body(
    amplitude, pair_irrep, fit_ac, fitting_tensor_bd, a_irrep, c_irrep, irrep_start, product, tile_len, tile_irrep
):
    fitting = jnp.transpose(fitting_tensor_bd, (1, 2, 0)).reshape(16, 25, 32, 256)
    fit = jnp.transpose(fit_ac, (1, 2, 0)).reshape(512, 256)
    pairs = pair_irrep.reshape(4, 128)
    a_row, len_row, irr_row = a_irrep.reshape(1, 64), tile_len.reshape(1, 64), tile_irrep.reshape(1, 64)
    def one_round(number, previous, first_round):
        number = jnp.asarray(number, jnp.int32).reshape(1)
        gathered = ladder(
            pair_irrep, a_irrep, c_irrep, irrep_start, product, tile_irrep, number, amplitude, fit, pairs, fitting)
        return place(pair_irrep, product, number, a_row, len_row, irr_row, gathered, previous, first_round)

    out, rounds = one_round(0, jnp.zeros((2, 64, 1024), F32), False)

    def more(carry):
        return carry[0] < rounds[0]

    def step(carry):
        number, out = carry
        return number + 1, one_round(number, out, False)[0]

    return lax.while_loop(more, step, (jnp.int32(1), out))[1]


def solution(mesh):
    placed = (
        P("idx", None, None),
        P(),
        P("con", None, None),
        P("con", "idx", None),
        P(),
        P(),
        P(),
        P(),
        P(),
        P(),
    )
    return jax.shard_map(
        body, mesh=mesh, in_specs=placed, out_specs=P(("idx", "con"), None, None), check_vma=False
    )
```

```python
import functools

import jax
import jax.numpy as jnp
from jax import lax
from jax.experimental import pallas as pl
from jax.experimental.pallas import tpu as pltpu
from jax.sharding import PartitionSpec as P

MESH = pl.DeviceIdType.MESH
BW = 16
NIRR = 8
WIN = 192
SLOTS = 16
NV = 800
KDIM = 8 * WIN
CUT = 256
F32 = jnp.float32
BF16 = jnp.bfloat16


def nt_dot(left, right):
    return lax.dot_general(left, right, (((1,), (1,)), ((), ())), preferred_element_type=F32)


def lookup(index, entries):
    out = jnp.zeros_like(index)
    for spot, entry in enumerate(entries):
        out = jnp.where(index == spot, entry, out)
    return out


def ladder_kernel(
    pair_s, airr_s, cirr_s, start_s, prod_s, tirr_s, round_s,
    amp_ref, a_ref, pairs_ref, f_hbm,
    out_ref,
    fv, x32, tc, tsend, trecv, ga, gb, asel, d_ref, rhs, rneed, acc, xf, xb, xr, zf, zb, vb,
    fsem, tsib_s, tsib_r, y_s, y_r, gz_s, gz_r, sib_s, sib_r, one_s, one_r, zg_s, zg_r, side_s, side_r, on_s, on_r,
    x_s, x_r, ze_s, ze_r,
):
    idx = lax.axis_index("idx")
    con = lax.axis_index("con")
    core = lax.rem(idx, 2)
    chip = idx // 2
    y = lax.rem(chip, 4)
    z = chip // 4
    sibling = (chip * 2 + 1 - core, con)

    def at_y(dy):
        return ((z * 4 + lax.rem(y + dy + 4, 4)) * 2 + core, con)

    def at_z(dz):
        return ((lax.rem(z + dz + 8, 8) * 4 + y) * 2 + core, con)

    def at_x(dx):
        return (idx, lax.rem(con + dx, 4))

    def remote(src, dst, send, recv, to):
        return pltpu.make_async_remote_copy(
            src_ref=src, dst_ref=dst, send_sem=send, recv_sem=recv, device_id=to, device_id_type=MESH)

    for b in range(16):
        pltpu.make_async_copy(f_hbm.at[b], fv.at[b], fsem.at[b]).start()

    barrier = pltpu.get_barrier_semaphore()
    peers = [sibling]
    for s in range(1, 8):
        there = lax.rem(z + s, 8) * 4 + y
        peers += [(there * 2 + core, con), (there * 2 + 1 - core, con)]
    for s in range(4):
        for dx in range(4):
            if s or dx:
                peers.append(((z * 4 + lax.rem(y + s, 4)) * 2 + core, lax.rem(con + dx, 4)))
    for peer in peers:
        pl.semaphore_signal(barrier, inc=1, device_id=peer, device_id_type=MESH)

    first = [jnp.minimum(start_s[g] // 32, (NV - WIN) // 32) for g in range(NIRR)]
    base = [first[g] * 32 for g in range(NIRR)]
    low = [start_s[g] - base[g] for g in range(NIRR)]
    high = [(start_s[g + 1] if g < 7 else NV) - base[g] for g in range(NIRR)]
    x32[:, 768:896] = jnp.zeros((64, 128), F32)
    x32[:, 0:NV] = amp_ref[...].astype(F32).reshape(64, NV)
    rows8 = lax.broadcasted_iota(jnp.int32, (8, 128), 0)
    target = []
    for p in range(8):
        irr = pair_s[idx * 8 + p]
        part = jnp.zeros((8, 128), jnp.int32)
        for c in range(8):
            part = jnp.where(rows8 == c, prod_s[irr, cirr_s[c]], part)
        target.append(part)
    target = jnp.concatenate(target, axis=0)
    target = jnp.concatenate([target, target], axis=1)
    lanes = lax.broadcasted_iota(jnp.int32, (64, 256), 1)
    window = jnp.zeros((64, 256), F32)
    whole = x32[...]
    for g in range(NIRR):
        moved = pltpu.roll(whole, 896 - base[g], 1)[:, 0:256]
        window = jnp.where((target == g) & (lanes >= low[g]) & (lanes < high[g]), moved, window)
    tc[0, :, :] = window[:, 0:128]
    tc[1, :, :] = window[:, 128:256]
    lane8 = lax.broadcasted_iota(jnp.int32, (8, 128), 1)
    for c in range(8):
        tsend[:, c * 128:(c + 1) * 128] = tc[0, pl.ds(c, 8, stride=8), :]
    for m in range(4):
        even = tc[1, pl.ds(2 * m, 8, stride=8), :]
        odd = pltpu.roll(tc[1, pl.ds(2 * m + 1, 8, stride=8), :], 64, 1)
        tsend[:, 1024 + m * 128:1024 + (m + 1) * 128] = jnp.where(lane8 < 64, even, odd)

    pl.semaphore_wait(barrier, len(peers))
    tcopy = remote(tsend, trecv, tsib_s, tsib_r, sibling)
    tcopy.start()

    tile = tirr_s[idx]
    prow = [[prod_s[i, j] for j in range(8)] for i in range(8)]
    ptile = [prod_s[i, tile] for i in range(8)]

    def factors():
        n = lax.broadcasted_iota(jnp.int32, (8, 512), 1)
        a_of, c_of = n // 8, lax.rem(n, 8)
        a_lane = lookup(a_of, [airr_s[a] for a in range(64)])
        c_lane = lookup(c_of, [cirr_s[c] for c in range(8)])
        a_rows = []
        for k in range(8):
            part = jnp.zeros((8, 128), jnp.int32)
            for i in range(8):
                part = jnp.where(rows8 == i, airr_s[k * 8 + i], part)
            a_rows.append(part)
        rank = jnp.zeros((8, 512), jnp.int32)
        for k in range(8):
            other = jnp.concatenate([a_rows[k]] * 4, axis=1)
            rank = rank + jnp.where(
                (other == a_lane) & (lax.broadcasted_iota(jnp.int32, (8, 512), 0) + k * 8 < a_of), 1, 0)
        rank = jnp.sum(rank, axis=0, keepdims=True) - round_s[0] * SLOTS
        block = lookup(lookup(a_lane, ptile) * 8 + c_lane, [e for row in prow for e in row])[0:1]
        code = jnp.where((rank >= 0) & (rank < SLOTS), block * 128 + c_of[0:1] * SLOTS + rank, -1)
        spot = lax.broadcasted_iota(jnp.int32, (128, 512), 0)
        for g in range(NIRR):
            pick = jnp.where(spot + g * 128 == code, 1.0, 0.0).astype(BF16)
            asel[g, :, :] = jnp.dot(pick, a_ref[...], preferred_element_type=F32).astype(BF16)

    def needs():
        need = lookup(lookup(pairs_ref[...], ptile), list(range(8))).astype(F32)
        eye = lax.broadcasted_iota(jnp.int32, (128, 128), 0) == lax.broadcasted_iota(jnp.int32, (128, 128), 1)
        for k in range(4):
            column = jnp.sum(jnp.where(eye, need[k:k + 1, :], 0.0), axis=1, keepdims=True)
            column = jnp.broadcast_to(column, (128, 128))
            rneed[2 * k, :, :] = column[0:64, :]
            rneed[2 * k + 1, :, :] = column[64:128, :]

    def integrals(begin, end):
        for b in range(begin, end):
            for g in range(NIRR):
                main = fv[b, pl.ds(first[g], 6), :, :].reshape(WIN, 256)
                tail = fv[b, pl.ds(first[g] + 4, 2), :, :].reshape(64, 256)
                got = nt_dot(asel[g], jnp.concatenate([main, tail], axis=0))
                d_ref[g, :, b * 16:(b + 1) * 16, :] = got.astype(BF16).reshape(8, 16, 256)

    def unit_a(dy):
        return ga.at[z, lax.rem(y + dy + 4, 4)]

    def group_a(dz):
        return ga.at[lax.rem(z + dz + 8, 8)]

    def unit(dz, dy):
        return gb.at[lax.rem(y + dy + 4, 4), lax.rem(z + dz + 8, 8)]

    away = (0, -1, 1, -2, 2, -3, 3, -4)

    def to_sibling(dz):
        slot = away.index(dz)
        return remote(group_a(dz), group_a(dz), sib_s.at[slot], sib_r.at[slot], sibling)

    def unit_to_sibling(dz, dy):
        slot, part = away.index(dz), unit(dz, dy)
        return remote(part, part, one_s.at[slot, dy % 4], one_r.at[slot, dy % 4], sibling)

    def along_y(s):
        return remote(unit_a(0), unit_a(0), y_s.at[s - 1], y_r.at[s - 1], at_y(s))

    def along_y_in(s):
        return remote(unit_a(-s), unit_a(-s), y_s.at[s - 1], y_r.at[s - 1], at_y(s))

    def groups_z(s):
        return remote(group_a(0), group_a(0), gz_s.at[s - 1], gz_r.at[s - 1], at_z(s))

    def groups_z_in(dz):
        s = (-dz) % 8
        return remote(group_a(dz), group_a(dz), gz_s.at[s - 1], gz_r.at[s - 1], at_z(s))

    def along_z(s):
        return remote(unit(0, 0), unit(0, 0), zg_s.at[s - 1], zg_r.at[s - 1], at_z(s))

    def along_z_in(dz):
        s = (-dz) % 8
        return remote(unit(dz, 0), unit(dz, 0), zg_s.at[s - 1], zg_r.at[s - 1], at_z(s))

    def side(dz, dy):
        slot, way = away.index(dz), (dy + 1) // 2
        part = unit(dz, 0)
        return remote(part, part, side_s.at[slot, way], side_r.at[slot, way], at_y(dy))

    def side_in(dz, dy):
        slot, way = away.index(dz), (dy + 1) // 2
        part = unit(dz, -dy)
        return remote(part, part, side_s.at[slot, way], side_r.at[slot, way], at_y(dy))

    def onward(dz):
        slot, dy = away.index(dz), (1 if dz % 2 == 0 else -1)
        part = unit(dz, -dy)
        return remote(part, part, on_s.at[slot], on_r.at[slot], at_y(dy))

    def onward_in(dz):
        slot, dy = away.index(dz), (1 if dz % 2 == 0 else -1)
        part = unit(dz, 2)
        return remote(part, part, on_s.at[slot], on_r.at[slot], at_y(dy))

    def route_a(stage):
        if stage == 0:
            for s in range(1, 4):
                along_y(s).start()
            return
        if stage == 1:
            for s in range(1, 4):
                along_y_in(s).wait_recv()
            for s in (1, 7, 2, 6, 3, 5, 4):
                groups_z(s).start()
            to_sibling(0).start()
            return
        if stage > 5:
            return
        for dz in both(stage - 1):
            groups_z_in(dz).wait_recv()
            to_sibling(dz).start()

    def both(far):
        return (-4,) if far == 4 else (0,) if far == 0 else (-far, far)

    def route_b(stage):
        arrive = {1: (-1, 1), 2: (-2, 2), 3: (-3, 3, -4)}
        pass_on = {1: (0,), 3: (-1, 1), 4: (-2, 2), 5: (-3, 3, -4)}
        take = {4: (0, -1, 1), 5: (-2, 2), 6: (-3, 3, -4)}
        if stage == 0:
            for s in (7, 1, 6, 2, 5, 3, 4):
                along_z(s).start()
            side(0, 1).start()
            side(0, -1).start()
            unit_to_sibling(0, 0).start()
        for dz in arrive.get(stage, ()):
            along_z_in(dz).wait_recv()
            side(dz, 1).start()
            side(dz, -1).start()
            unit_to_sibling(dz, 0).start()
        for dz in pass_on.get(stage, ()):
            dy = 1 if dz % 2 == 0 else -1
            side_in(dz, dy).wait_recv()
            onward(dz).start()
            unit_to_sibling(dz, -dy).start()
            side_in(dz, -dy).wait_recv()
            unit_to_sibling(dz, dy).start()
        for dz in take.get(stage, ()):
            onward_in(dz).wait_recv()
            unit_to_sibling(dz, 2).start()

    def gather(stage):
        @pl.when(core == 0)
        def _():
            route_a(stage)

        @pl.when(core == 1)
        def _():
            route_b(stage)

    factors()
    tcopy.wait()
    own, other = tsend[...], trecv[...]
    @pl.when(core == 0)
    def _():
        ga[z, y, :, :] = jnp.concatenate([own[:, 0:CUT], other[:, 0:CUT]], axis=0).astype(BF16)

    @pl.when(core == 1)
    def _():
        gb[y, z, :, :] = jnp.concatenate([other[:, CUT:KDIM], own[:, CUT:KDIM]], axis=0).astype(BF16)

    gather(0)
    needs()
    for b in range(16):
        pltpu.make_async_copy(f_hbm.at[b], fv.at[b], fsem.at[b]).wait()
    done = 0
    for stage, until in ((1, 4), (2, 8), (3, 11), (4, 14), (5, 16)):
        integrals(done, until)
        done = until
        gather(stage)

    lane256 = lax.broadcasted_iota(jnp.int32, (256, 128), 1)
    for r in range(NIRR):
        blocks = [prod_s[prod_s[r, tile], cirr_s[c]] for c in range(8)]
        for c in range(8):
            rhs[r, :, c * 128:(c + 1) * 128] = d_ref[blocks[c], c, :, 0:128]
        for m in range(4):
            even = d_ref[blocks[2 * m], 2 * m, :, 128:256]
            odd = d_ref[blocks[2 * m + 1], 2 * m + 1, :, 128:256]
            rhs[r, :, 1024 + m * 128:1024 + (m + 1) * 128] = jnp.where(lane256 < 64, even, odd)

    def from_sibling(part):
        @pl.when(core == 0)
        def _():
            for dz in part:
                for dy in range(4):
                    unit_to_sibling(dz, dy).wait_recv()

        @pl.when(core == 1)
        def _():
            for dz in part:
                to_sibling(dz).wait_recv()

    def give(h, to, dx):
        other = lax.rem(con + dx, 4)
        return remote(
            xb.at[h, to, other], xr.at[h, y, dx], x_s.at[h, to, dx], x_r.at[h, y, dx],
            ((z * 4 + to) * 2 + core, other))

    def given(h, src, dx):
        return remote(
            xb.at[h, src, con], xr.at[h, src, dx], x_s.at[h, src, dx], x_r.at[h, src, dx],
            ((z * 4 + src) * 2 + core, lax.rem(con + dx, 4)))

    parts = (away[0:4], away[4:8])
    for h in range(2):
        from_sibling(parts[h])
        places = [lax.rem(z + dz + 8, 8) for dz in parts[h]]
        left_side = jnp.concatenate(
            [jnp.concatenate([ga[zz].reshape(64, CUT) for zz in places], axis=0),
             jnp.concatenate([gb[:, zz, :, :].reshape(64, KDIM - CUT) for zz in places], axis=0)], axis=1)
        need = jnp.concatenate([rneed[zz, :, :] for zz in places], axis=0)
        for r in range(NIRR):
            if h == 0 and r == 6:
                gather(6)
            got = nt_dot(left_side, rhs[r])
            for k in range(2):
                part = got[:, k * 128:(k + 1) * 128]
                acc[k, :, :] = part if r == 0 else jnp.where(need == float(r), part, acc[k, :, :])
        for to in range(4):
            for r in range(4):
                for q in range(4):
                    for k in range(2):
                        xf[pl.ds(r * 32 + q * 2 + k, 4, stride=8), :] = acc[
                            k, pl.ds(to * 16 + (q // 2) * 8 + r * 2 + q % 2, 4, stride=64), :]
            xb[h, to, :, :, :] = xf[...].astype(BF16).reshape(4, 32, 128)
            for dx in range(1, 4):
                give(h, to, dx).start()

            @pl.when(y != to)
            def _():
                give(h, to, 0).start()

        xr[h, y, 0, :, :] = xb[h, y, con, :, :]

    def own_z(dz, flip):
        to = lax.rem(z + dz + 8, 8)
        kk = 1 - core if flip else core
        return remote(
            zb.at[to, kk], vb.at[core, z], ze_s.at[dz % 8, flip], ze_r.at[dz % 8, flip],
            ((to * 4 + y) * 2 + kk, con))

    def own_z_in(dz, flip):
        src = lax.rem(z + 8 - dz, 8)
        kk = 1 - core if flip else core
        return remote(
            zb.at[src, kk], vb.at[kk, src], ze_s.at[dz % 8, flip], ze_r.at[dz % 8, flip],
            ((src * 4 + y) * 2 + kk, con))

    routes = [(dz, flip) for dz in away for flip in (0, 1) if (dz, flip) != (0, 0)]
    for h in range(2):
        places = [lax.rem(z + dz + 8, 8) for dz in parts[h]]
        for src in range(4):
            @pl.when(y != src)
            def _():
                given(h, src, 0).wait_recv()

            for dx in range(1, 4):
                given(h, src, dx).wait_recv()
            total = (xr[h, src, 0].astype(F32) + xr[h, src, 1].astype(F32)) + (
                xr[h, src, 2].astype(F32) + xr[h, src, 3].astype(F32))
            for i in range(4):
                for k in range(2):
                    zf[i, k, src * 4:(src + 1) * 4, :] = total[i * 8 + k * 4:i * 8 + k * 4 + 4, :]
        for i in range(4):
            zb[places[i], :, :, :] = zf[i, :, :, :].astype(BF16)
        for dz, flip in routes:
            if dz in parts[h]:
                own_z(dz, flip).start()
    vb[core, z, :, :] = zb[z, core, :, :]
    for dz, flip in routes:
        own_z_in(dz, flip).wait_recv()
    out_ref[...] = vb[...]

    @pl.when(core == 0)
    def _():
        for s in range(1, 4):
            along_y(s).wait_send()
        for s in range(1, 8):
            groups_z(s).wait_send()
        for dz in away:
            to_sibling(dz).wait_send()

    @pl.when(core == 1)
    def _():
        for s in range(1, 8):
            along_z(s).wait_send()
        for dz in away:
            side(dz, 1).wait_send()
            side(dz, -1).wait_send()
            onward(dz).wait_send()
            for dy in range(4):
                unit_to_sibling(dz, dy).wait_send()

    for h in range(2):
        for to in range(4):
            for dx in range(1, 4):
                give(h, to, dx).wait_send()

            @pl.when(y != to)
            def _():
                give(h, to, 0).wait_send()

    for dz, flip in routes:
        own_z(dz, flip).wait_send()


def place_kernel(
    pair_s, prod_s, round_s, airr_ref, tlen_ref, tirr_ref, v_ref, prev_ref, out_ref, rounds_s, v32, left, expand, *, first_round
):
    idx = lax.axis_index("idx")
    con = lax.axis_index("con")
    lane16 = lax.broadcasted_iota(jnp.int32, (16, 128), 1)
    v32[...] = v_ref[...].reshape(2, 128, 128).astype(F32)
    for h in range(2):
        parts = []
        for pp in range(2):
            for kappa in range(2):
                parts.append(v32[kappa, pl.ds(pp * 2 + h, 32, stride=4), :])
        turned = jnp.concatenate(parts, axis=0).T
        for bl in range(8):
            piece = turned[bl * 16:(bl + 1) * 16, :]
            for pp in range(2):
                kept = jnp.where((lane16 // 64) == pp, piece, 0.0)
                left[pl.ds(pp * 16, 16), (h * 8 + bl) * 128:(h * 8 + bl + 1) * 128] = kept
    source = lax.broadcasted_iota(jnp.int32, (128, 1024), 0)
    lane = lax.broadcasted_iota(jnp.int32, (128, 1024), 1)
    local = lax.rem(source, 64)
    tile_first = (lax.rem(local, 32) * 2 + local // 32) * 16
    for b in range(16):
        expand[b * 128:(b + 1) * 128, :] = jnp.where(tile_first + b == lane, 1.0, 0.0).astype(BF16)
    a_row = airr_ref[...]
    row = lax.broadcasted_iota(jnp.int32, (64, 64), 0)
    col = lax.broadcasted_iota(jnp.int32, (64, 64), 1)
    a_col = jnp.sum(jnp.where(row == col, a_row, 0), axis=1, keepdims=True)
    rank = jnp.sum(jnp.where((a_col == a_row) & (col < row), 1, 0), axis=1, keepdims=True)
    rounds_s[0] = jnp.max(rank) // SLOTS + 1
    rank = rank - round_s[0] * SLOTS
    slot = lax.broadcasted_iota(jnp.int32, (64, 32), 1)
    full = left[...].astype(BF16)
    held = (rank >= 0) & (rank < SLOTS)
    pick = [jnp.where(held & (slot == rank + pp * 16), 1.0, 0.0) for pp in range(2)]
    pick = jnp.concatenate(pick, axis=0).astype(BF16)
    chosen = jnp.dot(pick, full, preferred_element_type=F32).astype(BF16)
    values = jnp.dot(chosen, expand[...], preferred_element_type=F32)
    spread = jnp.where(
        lax.broadcasted_iota(jnp.int32, (64, 1024), 0) == lax.broadcasted_iota(jnp.int32, (64, 1024), 1) // 16, 1.0, 0.0
    ).astype(BF16)

    def lanes_of(ref):
        wide = jnp.broadcast_to(ref[...], (8, 64)).astype(F32).astype(BF16)
        return jnp.dot(wide, spread, preferred_element_type=F32)[0:1]

    length, irrep = lanes_of(tlen_ref), lanes_of(tirr_ref).astype(jnp.int32)
    live = lax.rem(lax.broadcasted_iota(jnp.int32, (1, 1024), 1), 16).astype(F32) < length
    for pp in range(2):
        pair_irr = pair_s[idx * 8 + con * 2 + pp]
        need = lookup(irrep, [prod_s[pair_irr, i] for i in range(8)])
        need = jnp.where(live, need, -1)
        keep = a_col == need
        got = jnp.where(keep, values[pp * 64:(pp + 1) * 64, :], 0.0)
        if not first_round:
            got = got + prev_ref[pp, :, :]
        out_ref[pp, :, :] = got


def smem():
    return pl.BlockSpec(memory_space=pltpu.SMEM)


def vmem():
    return pl.BlockSpec(memory_space=pltpu.VMEM)


def ladder(pair_irrep, a_irrep, c_irrep, irrep_start, product, tile_irrep, number, amplitude, fit, pairs, fitting):
    dma = pltpu.SemaphoreType.DMA
    return pl.pallas_call(
        ladder_kernel,
        out_shape=jax.ShapeDtypeStruct((2, 8, 16, 128), BF16),
        in_specs=[smem()] * 7 + [vmem()] * 3 + [pl.BlockSpec(memory_space=pltpu.HBM)],
        out_specs=vmem(),
        scratch_shapes=[
            pltpu.VMEM((16, 25, 32, 256), BF16),
            pltpu.VMEM((64, 896), F32),
            pltpu.VMEM((2, 64, 128), F32),
            pltpu.VMEM((8, KDIM), F32),
            pltpu.VMEM((8, KDIM), F32),
            pltpu.VMEM((8, 4, 16, CUT), BF16),
            pltpu.VMEM((4, 8, 16, KDIM - CUT), BF16),
            pltpu.VMEM((NIRR, 128, 256), BF16),
            pltpu.VMEM((NIRR, 8, 256, 256), BF16),
            pltpu.VMEM((NIRR, 256, KDIM), BF16),
            pltpu.VMEM((8, 64, 128), F32),
            pltpu.VMEM((2, 256, 128), F32),
            pltpu.VMEM((128, 128), F32),
            pltpu.VMEM((2, 4, 4, 32, 128), BF16),
            pltpu.VMEM((2, 4, 4, 32, 128), BF16),
            pltpu.VMEM((4, 2, 16, 128), F32),
            pltpu.VMEM((8, 2, 16, 128), BF16),
            pltpu.VMEM((2, 8, 16, 128), BF16),
            dma((16,)), dma, dma, dma((3,)), dma((3,)), dma((7,)), dma((7,)),
            dma((8,)), dma((8,)), dma((8, 4)), dma((8, 4)), dma((7,)), dma((7,)), dma((8, 2)), dma((8, 2)), dma((8,)), dma((8,)),
            dma((2, 4, 4)), dma((2, 4, 4)), dma((8, 2)), dma((8, 2)),
        ],
        compiler_params=pltpu.CompilerParams(
            collective_id=0, has_side_effects=True, vmem_limit_bytes=48 * 1024 * 1024),
        name="ladder",
    )(pair_irrep, a_irrep, c_irrep, irrep_start, product, tile_irrep, number, amplitude, fit, pairs, fitting)


def place(pair_irrep, product, number, a_irrep, tile_len, tile_irrep, gathered, previous, first_round):
    return pl.pallas_call(
        functools.partial(place_kernel, first_round=first_round),
        out_shape=(jax.ShapeDtypeStruct((2, 64, 1024), F32), jax.ShapeDtypeStruct((1,), jnp.int32)),
        in_specs=[smem()] * 3 + [vmem()] * 5,
        out_specs=(vmem(), smem()),
        scratch_shapes=[pltpu.VMEM((2, 128, 128), F32), pltpu.VMEM((32, 2048), F32), pltpu.VMEM((2048, 1024), BF16)],
        compiler_params=pltpu.CompilerParams(vmem_limit_bytes=48 * 1024 * 1024),
        name="place" if first_round else "place_more",
    )(pair_irrep, product, number, a_irrep, tile_len, tile_irrep, gathered, previous)


def body(
    amplitude, pair_irrep, fit_ac, fitting_tensor_bd, a_irrep, c_irrep, irrep_start, product, tile_len, tile_irrep
):
    fitting = jnp.transpose(fitting_tensor_bd, (1, 2, 0)).reshape(16, 25, 32, 256)
    fit = jnp.transpose(fit_ac, (1, 2, 0)).reshape(512, 256)
    pairs = pair_irrep.reshape(4, 128)
    a_row, len_row, irr_row = a_irrep.reshape(1, 64), tile_len.reshape(1, 64), tile_irrep.reshape(1, 64)
    def one_round(number, previous, first_round):
        number = jnp.asarray(number, jnp.int32).reshape(1)
        gathered = ladder(
            pair_irrep, a_irrep, c_irrep, irrep_start, product, tile_irrep, number, amplitude, fit, pairs, fitting)
        return place(pair_irrep, product, number, a_row, len_row, irr_row, gathered, previous, first_round)

    out, rounds = one_round(0, jnp.zeros((2, 64, 1024), F32), False)

    def more(carry):
        return carry[0] < rounds[0]

    def step(carry):
        number, out = carry
        return number + 1, one_round(number, out, False)[0]

    return lax.while_loop(more, step, (jnp.int32(1), out))[1]


def solution(mesh):
    placed = (
        P("idx", None, None),
        P(),
        P("con", None, None),
        P("con", "idx", None),
        P(),
        P(),
        P(),
        P(),
        P(),
        P(),
    )
    return jax.shard_map(
        body, mesh=mesh, in_specs=placed, out_specs=P(("idx", "con"), None, None), check_vma=False
    )
```
